32 devices in a mesh: fsdp: 8 (over z, core), seq: 4 (over y, x).
Axes of the slice: x: 2, y: 2, z: 4, core: 2. Of those that a mesh axis runs over, the one named last changes fastest.
Arguments:
- tokens: bfloat16 [4096, 1536], P(('fsdp', 'seq')), may hold values from -6 to 6
- cotangent: bfloat16 [4096, 1536], P(('fsdp', 'seq')), may hold values from -6 to 6
- condition: bfloat16 [8, 1024], P('fsdp'), may hold values from -6 to 6
- caption: bfloat16 [2048, 4096], P('fsdp'), may hold values from -6 to 6
- positions: int32 [3, 4096], P(None, 'fsdp'), may hold values from 0 to 63
- clip_lengths: int32 [8], P('fsdp'), may hold values from 448 to 512, as said below
- caption_lengths: int32 [8], P('fsdp'), may hold values from 32 to 256, as said below
- modulator: bfloat16 [1024, 6144], P('fsdp', 'seq'), may hold values from -0.1875 to 0.1875
- query_weight: bfloat16 [1536, 1536], P('fsdp', 'seq'), may hold values from -0.15625 to 0.15625
- key_weight: bfloat16 [1536, 1536], P('fsdp', 'seq'), may hold values from -0.15625 to 0.15625
- value_weight: bfloat16 [1536, 1536], P('fsdp', 'seq'), may hold values from -0.15625 to 0.15625
- output_weight: bfloat16 [1536, 1536], P('seq', 'fsdp'), may hold values from -1.25 to 1.25
- textkey_weight: bfloat16 [4096, 1536], P('fsdp', 'seq'), may hold values from -0.09375 to 0.09375
- textvalue_weight: bfloat16 [4096, 1536], P('fsdp', 'seq'), may hold values from -0.09375 to 0.09375
- gate_weight: bfloat16 [1536, 4096], P('fsdp', 'seq'), may hold values from -0.15625 to 0.15625
- up_weight: bfloat16 [1536, 4096], P('fsdp', 'seq'), may hold values from -0.15625 to 0.15625
- down_weight: bfloat16 [4096, 1536], P('seq', 'fsdp'), may hold values from -0.09375 to 0.09375
- attn_gain: float32 [1536], replicated, may hold values from 0.5 to 1.5
- ffn_gain: float32 [1536], replicated, may hold values from 0.5 to 1.5
- query_gain: float32 [64], replicated, may hold values from 0.5 to 1.5
- key_gain: float32 [64], replicated, may hold values from 0.5 to 1.5
- cross_gate: float32 [24], replicated, may hold values from -1.5 to 1.5
Outputs:
- block_out: bfloat16 [4096, 1536], P(('fsdp', 'seq'))
- token_grad: float32 [4096, 1536], P(('fsdp', 'seq'))
- modulator_grad: float32 [1024, 6144], P('fsdp', 'seq')
- query_grad: float32 [1536, 1536], P('fsdp', 'seq')
- key_grad: float32 [1536, 1536], P('fsdp', 'seq')
- value_grad: float32 [1536, 1536], P('fsdp', 'seq')
- output_grad: float32 [1536, 1536], P('seq', 'fsdp')
- textkey_grad: float32 [4096, 1536], P('fsdp', 'seq')
- textvalue_grad: float32 [4096, 1536], P('fsdp', 'seq')
- gate_grad: float32 [1536, 4096], P('fsdp', 'seq')
- up_grad: float32 [1536, 4096], P('fsdp', 'seq')
- down_grad: float32 [4096, 1536], P('seq', 'fsdp')
- attn_gain_grad: float32 [1536], replicated
- ffn_gain_grad: float32 [1536], replicated
- query_gain_grad: float32 [64], replicated
- key_gain_grad: float32 [64], replicated
- cross_gate_grad: float32 [24], replicated
- residual_rms: float32 [3, 8], P(None, 'fsdp')
The draws below stay inside these ranges and needn't reach their ends.
Inputs may be any that keep to these rules, and one draw needn't show every extreme that they name: `clip_lengths`: each clip's valid tokens are its first slots; some clip is full and some clip has exactly the least length. `caption_lengths`: each caption's valid tokens are its first slots; some caption is full and some has exactly the least length.
All inputs are finite; a program needn't handle non-finite values.
Results may differ from the reference program's by a relative error of at most 0.019.
Values may be sent and summed in bfloat16 or wider, within the bound.
No kernel may reach another device: no remote copies, remote signals or barrier semaphores. Data moves between devices by JAX's collectives and lax.ppermute only.
A program may use at most 128 MiB of HBM per device.

```python
import math
import jax
import jax.numpy as jnp
from jax import lax

D = 1536
HEADS = 24
HEAD = 64
FF = 4096
CAPW = 4096
ADA = 1024
CAP = 256
TOK_DEV = 128
CLIP = 512
CLIPS = 8
TOKENS = 4096
N_SEQ = 4


def draw_clip_lengths(key, part):
    key = jax.random.fold_in(key, 11)
    short_key, order_key = jax.random.split(key)
    shortfall = jax.random.randint(short_key, (CLIPS,), 0, TOK_DEV // 2 + 1)
    order = jax.random.permutation(order_key, CLIPS)
    lengths = CLIP - shortfall
    lengths = jnp.where(jnp.arange(CLIPS) == order[0], CLIP, lengths)
    lengths = jnp.where(jnp.arange(CLIPS) == order[1], CLIP - TOK_DEV // 2, lengths)
    return lengths.astype(jnp.int32)


def draw_caption_lengths(key, part):
    key = jax.random.fold_in(key, 23)
    length_key, order_key = jax.random.split(key)
    lengths = jax.random.randint(length_key, (CLIPS,), CAP // 8, CAP + 1)
    order = jax.random.permutation(order_key, CLIPS)
    lengths = jnp.where(jnp.arange(CLIPS) == order[0], CAP, lengths)
    lengths = jnp.where(jnp.arange(CLIPS) == order[1], CAP // 8, lengths)
    return lengths.astype(jnp.int32)


def set_ends(values, stream_key, least, top_value):
    dims = values.shape
    index_at = [jax.random.randint(jax.random.fold_in(stream_key, axis), (), 0, dims[axis]) for axis in range(len(dims))]
    values = values.at[tuple(index_at)].set(least)
    longest = dims.index(max(dims))
    index_at[longest] = (index_at[longest] + 1) % dims[longest]
    return values.at[tuple(index_at)].set(top_value)


def levels(rng, extent, cuts, low, high):
    def one(position, blocks):
        heights = jax.random.uniform(jax.random.fold_in(jax.random.fold_in(rng, 6), position), (blocks,), jnp.float32, low / len(cuts), high / len(cuts))
        return jnp.repeat(jnp.exp(heights), extent[position] // blocks).reshape((-1,) + (1,) * (len(extent) - position - 1))

    level = one(*cuts[0])
    for cut in cuts[1:]:
        level = level * one(*cut)
    return level


def normal_values(key, shape, deviation, reach, cuts=(), kind=jnp.bfloat16):
    factor_of = levels(key, shape, cuts, -0.22, 0.18) if cuts else 1.0
    drawn = jax.random.normal(key, shape, jnp.float32) * deviation * factor_of
    return jnp.minimum(jnp.maximum(drawn, -reach), reach).astype(kind)


def setup_inputs(seed: int = 0) -> dict:
    seeds = jax.random.split(jax.random.key(seed), 23)
    tokens = normal_values(seeds[0], (TOKENS, D), 1.0, 6.0, ((0, 32),))
    cotangent = normal_values(seeds[1], (TOKENS, D), 1.0, 6.0, ((0, 32),))
    condition = normal_values(seeds[2], (CLIPS, ADA), 1.0, 6.0, ((0, 8),))
    caption = normal_values(seeds[3], (CLIPS * CAP, CAPW), 1.0, 6.0, ((0, 8),))
    positions = set_ends(jax.random.randint(seeds[4], (3, TOKENS), 0, 64), jax.random.fold_in(seeds[4], 1), 0, 63).astype(jnp.int32)
    clip_lengths = draw_clip_lengths(jax.random.fold_in(seeds[22], 71), 0)
    caption_lengths = draw_caption_lengths(jax.random.fold_in(seeds[22], 71), 0)
    modulator = normal_values(seeds[7], (ADA, 4 * D), ADA ** -0.5, 0.1875, ((0, 8), (1, 4)))
    query_weight = normal_values(seeds[8], (D, D), D ** -0.5, 0.15625, ((0, 8), (1, 4)))
    key_weight = normal_values(seeds[9], (D, D), D ** -0.5, 0.15625, ((0, 8), (1, 4)))
    value_weight = normal_values(seeds[10], (D, D), D ** -0.5, 0.15625, ((0, 8), (1, 4)))
    output_weight = normal_values(seeds[11], (D, D), (max(1, D * 8 // (TOK_DEV * N_SEQ))) ** -0.5, 1.25, ((0, 4), (1, 8)))
    textkey_weight = normal_values(seeds[12], (CAPW, D), CAPW ** -0.5, 0.09375, ((0, 8), (1, 4)))
    textvalue_weight = normal_values(seeds[13], (CAPW, D), CAPW ** -0.5, 0.09375, ((0, 8), (1, 4)))
    gate_weight = normal_values(seeds[14], (D, FF), D ** -0.5, 0.15625, ((0, 8), (1, 4)))
    up_weight = normal_values(seeds[15], (D, FF), D ** -0.5, 0.15625, ((0, 8), (1, 4)))
    down_weight = normal_values(seeds[16], (FF, D), FF ** -0.5, 0.09375, ((0, 4), (1, 8)))
    attn_gain = jnp.clip(1.0 + 0.1 * jax.random.normal(seeds[17], (D,), jnp.float32), 0.5, 1.5)
    ffn_gain = jnp.clip(1.0 + 0.1 * jax.random.normal(seeds[18], (D,), jnp.float32), 0.5, 1.5)
    query_gain = jnp.clip(1.0 + 0.1 * jax.random.normal(seeds[19], (HEAD,), jnp.float32), 0.5, 1.5)
    key_gain = jnp.clip(1.0 + 0.1 * jax.random.normal(seeds[20], (HEAD,), jnp.float32), 0.5, 1.5)
    cross_gate = jnp.clip(jax.random.uniform(seeds[21], (HEADS,), jnp.float32, -1.5, 1.5), -1.5, 1.5)
    return dict(tokens=tokens, cotangent=cotangent, condition=condition, caption=caption, positions=positions, clip_lengths=clip_lengths, caption_lengths=caption_lengths, modulator=modulator, query_weight=query_weight, key_weight=key_weight, value_weight=value_weight, output_weight=output_weight, textkey_weight=textkey_weight, textvalue_weight=textvalue_weight, gate_weight=gate_weight, up_weight=up_weight, down_weight=down_weight, attn_gain=attn_gain, ffn_gain=ffn_gain, query_gain=query_gain, key_gain=key_gain, cross_gate=cross_gate)


epsilon = 1e-06
masked_score = -1e+30

@jax.custom_vjp
def low(v):
    return lax.optimization_barrier(v.astype(jnp.bfloat16)).astype(jnp.float32)

@jax.custom_vjp
def low_back(v):
    return v

def low_keep(v):
    return (low(v), None)

def low_pass(kept, grad):
    return (grad,)

def back_keep(v):
    return (v, None)

def back_low(kept, grad):
    return (low(grad),)
low.defvjp(low_keep, low_pass)
low_back.defvjp(back_keep, back_low)

def rope_tables(positions, head_size):
    half = head_size // 2
    pair_index = jnp.arange(half)
    frequency = jnp.exp(pair_index.astype(jnp.float32) * (-2.0 * math.log(10000.0) / head_size))
    angle = jnp.zeros((positions.shape[1], half), jnp.float32)
    for axis_number in range(3):
        chosen = jnp.where(pair_index % 3 == axis_number, frequency, jnp.zeros_like(frequency))
        angle = angle + positions[axis_number].astype(jnp.float32)[:, None] * chosen[None, :]
    return (jnp.cos(angle), jnp.sin(angle))

def rotate(values, cosine, sine):
    half = values.shape[-1] // 2
    first = values[..., :half]
    second = values[..., half:]
    return jnp.concatenate([first * cosine - second * sine, first * sine + second * cosine], axis=-1)

def head_norm(values, gain):
    return values * lax.rsqrt(lax.optimization_barrier(jnp.mean(values * values, axis=-1, keepdims=True)) + epsilon) * gain

def softmax_rows(scores):
    peak = lax.optimization_barrier(jnp.max(scores, axis=-1, keepdims=True))
    expo = jnp.exp(scores - peak)
    return expo / lax.optimization_barrier(jnp.sum(expo, axis=-1, keepdims=True))

def project(left, right):
    return jnp.dot(left, right, precision=lax.Precision.HIGHEST)

def clip_forward(params, inputs, condition, caption, positions, length, text_length):
    modulator, query_weight, key_weight, value_weight, output_weight, textkey_weight, textvalue_weight, gate_weight, up_weight, down_weight, attn_gain, ffn_gain, query_gain, key_gain, cross_gate = params
    highest = lax.Precision.HIGHEST
    rows = inputs.shape[0]
    width = inputs.shape[1]
    scale = HEAD ** (-0.5)
    modulation = low_back(project(low(jax.nn.silu(condition))[None, :], modulator))[0]
    scale_attn = modulation[:width]
    gate_attn = modulation[width:2 * width]
    scale_ffn = modulation[2 * width:3 * width]
    gate_ffn = modulation[3 * width:]
    unit_attn = inputs * lax.rsqrt(lax.optimization_barrier(jnp.mean(inputs * inputs, axis=-1, keepdims=True)) + epsilon)
    normed = low(unit_attn * attn_gain * (1.0 + scale_attn))
    query_raw = low_back(project(normed, query_weight)).reshape(rows, HEADS, HEAD)
    key_raw = low_back(project(normed, key_weight)).reshape(rows, HEADS, HEAD)
    value_heads = low(low_back(project(normed, value_weight))).reshape(rows, HEADS, HEAD)
    cosine, sine = rope_tables(positions, HEAD)
    cosine = cosine[:, None, :]
    sine = sine[:, None, :]
    query_rot = low(rotate(head_norm(query_raw, query_gain), cosine, sine))
    key_rot = low(rotate(head_norm(key_raw, key_gain), cosine, sine))
    key_valid = (jnp.arange(rows) < length)[None, None, :]
    scores = jnp.einsum('qhd,khd->hqk', query_rot, key_rot, precision=highest) * scale
    scores = jnp.where(key_valid, low_back(scores), masked_score)
    self_out = jnp.einsum('hqk,khd->qhd', low(softmax_rows(scores)), value_heads, precision=highest)
    textkey = low(low_back(project(caption, textkey_weight))).reshape(CAP, HEADS, HEAD)
    textvalue = low(low_back(project(caption, textvalue_weight))).reshape(CAP, HEADS, HEAD)
    text_valid = (jnp.arange(CAP) < text_length)[None, None, :]
    cross_scores = jnp.einsum('qhd,khd->hqk', query_rot, textkey, precision=highest) * scale
    cross_scores = jnp.where(text_valid, low_back(cross_scores), masked_score)
    cross_out = low_back(jnp.einsum('hqk,khd->qhd', low(softmax_rows(cross_scores)), textvalue, precision=highest))
    mixed = self_out + jnp.tanh(cross_gate)[None, :, None] * cross_out
    mixed_rows = low(low_back(mixed)).reshape(rows, width)
    attn_out = low_back(project(mixed_rows, output_weight))
    branch_attn = jnp.tanh(gate_attn) * attn_out
    hidden_in = inputs + branch_attn
    unit_ffn = hidden_in * lax.rsqrt(lax.optimization_barrier(jnp.mean(hidden_in * hidden_in, axis=-1, keepdims=True)) + epsilon)
    ffn_in = low(unit_ffn * ffn_gain * (1.0 + scale_ffn))
    gate_act = low_back(project(ffn_in, gate_weight))
    up_act = low_back(project(ffn_in, up_weight))
    hidden = low(jax.nn.silu(gate_act) * up_act)
    branch_ffn = jnp.tanh(gate_ffn) * low_back(project(hidden, down_weight))
    result = hidden_in + branch_ffn
    row_valid = (jnp.arange(rows) < length)[:, None]
    first_sum = jnp.sum(jnp.where(row_valid, result * result, 0.0))
    second_sum = jnp.sum(jnp.where(row_valid, branch_attn * branch_attn, 0.0))
    third_sum = jnp.sum(jnp.where(row_valid, branch_ffn * branch_ffn, 0.0))
    sums = jnp.stack([first_sum, second_sum, third_sum])
    stats = jnp.sqrt(sums / (length.astype(jnp.float32) * width))
    return (result, stats)

def reference(tokens, cotangent, condition, caption, positions, clip_lengths, caption_lengths, modulator, query_weight, key_weight, value_weight, output_weight, textkey_weight, textvalue_weight, gate_weight, up_weight, down_weight, attn_gain, ffn_gain, query_gain, key_gain, cross_gate):
    params = tuple((weight.astype(jnp.float32) for weight in (modulator, query_weight, key_weight, value_weight, output_weight, textkey_weight, textvalue_weight, gate_weight, up_weight, down_weight, attn_gain, ffn_gain, query_gain, key_gain, cross_gate)))
    clip_tokens = tokens.astype(jnp.float32).reshape(CLIPS, CLIP, D)
    clip_cond = condition.astype(jnp.float32)
    clip_caption = caption.astype(jnp.float32).reshape(CLIPS, CAP, CAPW)
    clip_positions = positions.reshape(3, CLIPS, CLIP).transpose(1, 0, 2)

    def forward(token_blocks, weights):

        def one_clip(inputs):
            return clip_forward(weights, inputs[0], inputs[1], inputs[2], inputs[3], inputs[4], inputs[5])
        return lax.map(jax.checkpoint(one_clip), (token_blocks, clip_cond, clip_caption, clip_positions, clip_lengths, caption_lengths))
    result, pullback, stats = jax.vjp(forward, clip_tokens, params, has_aux=True)
    grad_tokens, grads = pullback(cotangent.astype(jnp.float32).reshape(CLIPS, CLIP, D))
    return (result.reshape(TOKENS, D).astype(jnp.bfloat16), grad_tokens.reshape(TOKENS, D), grads[0], grads[1], grads[2], grads[3], grads[4], grads[5], grads[6], grads[7], grads[8], grads[9], grads[10], grads[11], grads[12], grads[13], grads[14], stats.T)
```

```python
import math

import jax
import jax.numpy as jnp
from jax import lax
from jax.sharding import PartitionSpec as P

epsilon = 1e-06
masked_score = -1e30
f32 = jnp.float32
bf16 = jnp.bfloat16


def rope_tables(positions, head_size):
    half = head_size // 2
    pair_index = jnp.arange(half)
    frequency = jnp.exp(pair_index.astype(f32) * (-2.0 * math.log(10000.0) / head_size))
    angle = jnp.zeros((positions.shape[1], half), f32)
    for axis_number in range(3):
        chosen = jnp.where(pair_index % 3 == axis_number, frequency, jnp.zeros_like(frequency))
        angle = angle + positions[axis_number].astype(f32)[:, None] * chosen[None, :]
    return (jnp.cos(angle), jnp.sin(angle))


def rotate(values, cosine, sine):
    half = values.shape[-1] // 2
    first = values[..., :half]
    second = values[..., half:]
    return jnp.concatenate(
        [first * cosine - second * sine, first * sine + second * cosine], axis=-1
    )


def unrotate(grads, cosine, sine):
    half = grads.shape[-1] // 2
    first = grads[..., :half]
    second = grads[..., half:]
    return jnp.concatenate(
        [first * cosine + second * sine, second * cosine - first * sine], axis=-1
    )


def head_norm(values, gain):
    inverse = lax.rsqrt(jnp.mean(values * values, axis=-1, keepdims=True) + epsilon)
    unit = values * inverse
    return (unit * gain, unit, inverse)


def head_norm_back(grads, unit, inverse, gain):
    gain_grad = jnp.sum(grads * unit, axis=(0, 1))
    scaled = grads * gain
    return (inverse * (scaled - unit * jnp.mean(scaled * unit, axis=-1, keepdims=True)), gain_grad)


def dot(left, right):
    return jnp.dot(left, right, preferred_element_type=f32)


def dot_nt(left, right):
    return lax.dot_general(left, right, (((1,), (1,)), ((), ())), preferred_element_type=f32)


def dot_tn(left, right):
    return lax.dot_general(left, right, (((0,), (0,)), ((), ())), preferred_element_type=f32)


def build(n_f, n_s):
    swaps = [[(i, i ^ k) for i in range(n_s)] for k in range(n_s)]

    def seq_gather(block):
        parts = [block] + [lax.ppermute(block, "seq", swaps[k]) for k in range(1, n_s)]
        return jnp.concatenate(parts, axis=0)

    def seq_scatter(total, rows):
        parts = [
            lax.ppermute(total[k * rows : (k + 1) * rows].astype(bf16), "seq", swaps[k])
            for k in range(1, n_s)
        ]
        result = total[:rows]
        for part in parts:
            result = result + part.astype(f32)
        return result

    def fsdp_gather(shard):
        return lax.all_gather(shard, "fsdp", axis=0, tiled=True)

    def fsdp_scatter(total):
        return lax.psum_scatter(total, "fsdp", scatter_dimension=0, tiled=True).astype(f32)

    def local(
        tokens,
        cotangent,
        condition,
        caption,
        positions,
        clip_lengths,
        caption_lengths,
        modulator,
        query_weight,
        key_weight,
        value_weight,
        output_weight,
        textkey_weight,
        textvalue_weight,
        gate_weight,
        up_weight,
        down_weight,
        attn_gain,
        ffn_gain,
        query_gain,
        key_gain,
        cross_gate,
    ):
        rows = tokens.shape[0]
        width = tokens.shape[1]
        head_size = query_gain.shape[0]
        columns = query_weight.shape[1]
        heads = columns // head_size
        units = gate_weight.shape[1]
        clip_rows = positions.shape[1]
        text_rows = caption.shape[0]
        seq_index = lax.axis_index("seq")
        fsdp_index = lax.axis_index("fsdp")
        length = clip_lengths[0]
        text_length = caption_lengths[0]
        scale = head_size ** (-0.5)

        attn_full = fsdp_gather(
            jnp.concatenate([query_weight, key_weight, value_weight, output_weight.T], axis=1)
        )
        text_full = fsdp_gather(jnp.concatenate([textkey_weight, textvalue_weight], axis=1))
        ffn_full = fsdp_gather(jnp.concatenate([gate_weight, up_weight, down_weight.T], axis=1))

        tokens_all = seq_gather(tokens).astype(f32)
        cotangent_all = seq_gather(cotangent).astype(f32)

        cond_low = jax.nn.silu(condition.astype(f32)).astype(bf16)
        cond_all = lax.all_gather(cond_low, "fsdp", axis=0, tiled=True)
        mod_rows = modulator.shape[0]
        cond_mine = lax.dynamic_slice_in_dim(cond_all, fsdp_index * mod_rows, mod_rows, 1)
        mod_part = dot(cond_mine, modulator)
        mod_part = lax.psum_scatter(mod_part, "fsdp", scatter_dimension=0, tiled=True)
        modulation = lax.all_gather(mod_part, "seq", axis=1, tiled=True)[0]
        scale_attn = modulation[:width]
        gate_attn = modulation[width : 2 * width]
        scale_ffn = modulation[2 * width : 3 * width]
        gate_ffn = modulation[3 * width :]
        tanh_attn = jnp.tanh(gate_attn)
        tanh_ffn = jnp.tanh(gate_ffn)

        order = [seq_index ^ k for k in range(n_s)]
        row_index = jnp.concatenate([order[k] * rows + jnp.arange(rows) for k in range(n_s)])
        places = jnp.concatenate(
            [lax.dynamic_slice_in_dim(positions, order[k] * rows, rows, 1) for k in range(n_s)],
            axis=1,
        )

        inv_attn_all = lax.rsqrt(jnp.mean(tokens_all * tokens_all, axis=-1, keepdims=True) + epsilon)
        normed_all = (tokens_all * inv_attn_all * attn_gain * (1.0 + scale_attn)).astype(bf16)
        inputs = tokens.astype(f32)
        inv_attn = inv_attn_all[:rows]
        unit_attn = inputs * inv_attn
        qkv = dot(normed_all, attn_full[:, : 3 * columns])
        query_raw = qkv[:, :columns].reshape(clip_rows, heads, head_size)
        key_raw = qkv[:, columns : 2 * columns].reshape(clip_rows, heads, head_size)
        value_heads = (
            qkv[:, 2 * columns :].astype(bf16).reshape(clip_rows, heads, head_size).transpose(1, 0, 2)
        )
        cosine, sine = rope_tables(places, head_size)
        cosine = cosine[:, None, :]
        sine = sine[:, None, :]
        query_normed, query_unit, query_inverse = head_norm(query_raw, query_gain)
        key_normed, key_unit, key_inverse = head_norm(key_raw, key_gain)
        query_heads = rotate(query_normed, cosine, sine).astype(bf16).transpose(1, 0, 2)
        key_heads = rotate(key_normed, cosine, sine).astype(bf16).transpose(1, 0, 2)
        key_valid = (row_index < length)[None, None, :]

        def softmax(scores):
            peak = jnp.max(scores, axis=-1, keepdims=True)
            expo = jnp.exp(scores - peak)
            return expo / jnp.sum(expo, axis=-1, keepdims=True)

        def bmm(spec, left, right):
            return jnp.einsum(spec, left, right, preferred_element_type=f32)

        scores = bmm("hqd,hkd->hqk", query_heads, key_heads) * scale
        probs = softmax(jnp.where(key_valid, scores, masked_score))
        probs_low = probs.astype(bf16)
        self_out = bmm("hqk,hkd->hqd", probs_low, value_heads)
        text_both = dot(caption, text_full).astype(bf16)
        textkey_heads = text_both[:, :columns].reshape(text_rows, heads, head_size).transpose(1, 0, 2)
        textvalue_heads = (
            text_both[:, columns:].reshape(text_rows, heads, head_size).transpose(1, 0, 2)
        )
        text_valid = (jnp.arange(text_rows) < text_length)[None, None, :]
        cross_scores = bmm("hqd,hkd->hqk", query_heads, textkey_heads) * scale
        cross_probs = softmax(jnp.where(text_valid, cross_scores, masked_score))
        cross_low = cross_probs.astype(bf16)
        cross_out = bmm("hqk,hkd->hqd", cross_low, textvalue_heads)
        gate_heads = jnp.tanh(lax.dynamic_slice_in_dim(cross_gate, seq_index * heads, heads))
        mixed_heads = self_out + gate_heads[:, None, None] * cross_out
        mixed_rows = mixed_heads.transpose(1, 0, 2).reshape(clip_rows, columns).astype(bf16)
        output_t = attn_full[:, 3 * columns :]
        attn_out = seq_scatter(dot_nt(mixed_rows, output_t), rows)
        branch_attn = tanh_attn * attn_out
        hidden_in = inputs + branch_attn
        inv_ffn = lax.rsqrt(jnp.mean(hidden_in * hidden_in, axis=-1, keepdims=True) + epsilon)
        unit_ffn = hidden_in * inv_ffn
        ffn_in = (unit_ffn * ffn_gain * (1.0 + scale_ffn)).astype(bf16)
        ffn_all = seq_gather(ffn_in)
        act = dot(ffn_all, ffn_full[:, : 2 * units])
        gate_act = act[:, :units]
        up_act = act[:, units:]
        down_t = ffn_full[:, 2 * units :]
        sigmoid_gate = jax.nn.sigmoid(gate_act)
        silu_gate = gate_act * sigmoid_gate
        hidden = (silu_gate * up_act).astype(bf16)
        ffn_back_all = (tanh_ffn * cotangent_all).astype(bf16)
        grad_hidden = dot(ffn_back_all, down_t)
        grad_gate_act = (
            grad_hidden * up_act * sigmoid_gate * (1.0 + gate_act * (1.0 - sigmoid_gate))
        ).astype(bf16)
        grad_up_act = (grad_hidden * silu_gate).astype(bf16)
        grad_act = jnp.concatenate([grad_gate_act, grad_up_act], axis=1)
        grad_ffn_in = seq_scatter(dot_nt(grad_act, ffn_full[:, : 2 * units]), rows)

        ffn_out = seq_scatter(dot_nt(hidden, down_t), rows)
        ffn_part = jnp.concatenate(
            [dot_tn(ffn_all, grad_act).astype(bf16), dot_tn(ffn_back_all, hidden).astype(bf16)], axis=1
        )
        ffn_grads = fsdp_scatter(ffn_part)

        branch_ffn = tanh_ffn * ffn_out
        result = hidden_in + branch_ffn
        row_valid = (seq_index * rows + jnp.arange(rows) < length)[:, None]
        sums = jnp.stack(
            [
                jnp.sum(jnp.where(row_valid, result * result, 0.0)),
                jnp.sum(jnp.where(row_valid, branch_attn * branch_attn, 0.0)),
                jnp.sum(jnp.where(row_valid, branch_ffn * branch_ffn, 0.0)),
            ]
        )
        grad_out = cotangent.astype(f32)
        grad_gate_ffn = jnp.sum(grad_out * ffn_out, axis=0) * (1.0 - tanh_ffn * tanh_ffn)

        grad_ffn_gain = jnp.sum(grad_ffn_in * unit_ffn * (1.0 + scale_ffn), axis=0)
        grad_scale_ffn = jnp.sum(grad_ffn_in * unit_ffn * ffn_gain, axis=0)
        scaled_ffn = grad_ffn_in * ffn_gain * (1.0 + scale_ffn)
        grad_hidden_in = grad_out + inv_ffn * (
            scaled_ffn - unit_ffn * jnp.mean(scaled_ffn * unit_ffn, axis=-1, keepdims=True)
        )
        attn_back = (tanh_attn * grad_hidden_in).astype(bf16)
        grad_gate_attn = jnp.sum(grad_hidden_in * attn_out, axis=0) * (1.0 - tanh_attn * tanh_attn)
        attn_back_all = seq_gather(attn_back)
        output_part = dot_tn(attn_back_all, mixed_rows).astype(bf16)
        grad_mixed = dot(attn_back_all, output_t).astype(bf16)
        grad_mixed = grad_mixed.reshape(clip_rows, heads, head_size).transpose(1, 0, 2)
        grad_mixed_wide = grad_mixed.astype(f32)
        grad_gate_heads = jnp.sum(grad_mixed_wide * cross_out, axis=(1, 2)) * (
            1.0 - gate_heads * gate_heads
        )
        cross_back = (gate_heads[:, None, None] * grad_mixed_wide).astype(bf16)
        grad_cross_probs = bmm("hqd,hkd->hqk", cross_back, textvalue_heads)
        cross_delta = jnp.sum(cross_probs * grad_cross_probs, axis=-1, keepdims=True)
        grad_cross_scores = (cross_probs * (grad_cross_probs - cross_delta)).astype(bf16)
        grad_query_cross = bmm("hqk,hkd->hqd", grad_cross_scores, textkey_heads) * scale
        grad_textkey = bmm("hqk,hqd->hkd", grad_cross_scores, query_heads) * scale
        grad_textvalue = bmm("hqk,hqd->hkd", cross_low, cross_back)

        grad_probs = bmm("hqd,hkd->hqk", grad_mixed, value_heads)
        delta = jnp.sum(probs * grad_probs, axis=-1, keepdims=True)
        grad_scores = (probs * (grad_probs - delta)).astype(bf16)
        grad_query_heads = grad_query_cross + bmm("hqk,hkd->hqd", grad_scores, key_heads) * scale
        grad_key_heads = bmm("hqk,hqd->hkd", grad_scores, query_heads) * scale
        grad_value_heads = bmm("hqk,hqd->hkd", probs_low, grad_mixed)

        grad_query_normed = unrotate(grad_query_heads.transpose(1, 0, 2), cosine, sine)
        grad_key_normed = unrotate(grad_key_heads.transpose(1, 0, 2), cosine, sine)
        grad_query_raw, grad_query_gain = head_norm_back(
            grad_query_normed, query_unit, query_inverse, query_gain
        )
        grad_key_raw, grad_key_gain = head_norm_back(
            grad_key_normed, key_unit, key_inverse, key_gain
        )
        qkv_rows = jnp.concatenate(
            [
                grad_query_raw.reshape(clip_rows, columns).astype(bf16),
                grad_key_raw.reshape(clip_rows, columns).astype(bf16),
                grad_value_heads.transpose(1, 0, 2).reshape(clip_rows, columns).astype(bf16),
            ],
            axis=1,
        )
        text_grads_rows = jnp.concatenate(
            [
                grad_textkey.transpose(1, 0, 2).reshape(text_rows, columns).astype(bf16),
                grad_textvalue.transpose(1, 0, 2).reshape(text_rows, columns).astype(bf16),
            ],
            axis=1,
        )
        text_grads = fsdp_scatter(dot_tn(caption, text_grads_rows).astype(bf16))
        attn_grads = fsdp_scatter(
            jnp.concatenate([dot_tn(normed_all, qkv_rows).astype(bf16), output_part], axis=1)
        )
        grad_normed = seq_scatter(dot_nt(qkv_rows, attn_full[:, : 3 * columns]), rows)
        grad_attn_gain = jnp.sum(grad_normed * unit_attn * (1.0 + scale_attn), axis=0)
        grad_scale_attn = jnp.sum(grad_normed * unit_attn * attn_gain, axis=0)
        scaled_attn = grad_normed * attn_gain * (1.0 + scale_attn)
        token_grad = grad_hidden_in + inv_attn * (
            scaled_attn - unit_attn * jnp.mean(scaled_attn * unit_attn, axis=-1, keepdims=True)
        )

        gate_heads_full = lax.dynamic_update_slice_in_dim(
            jnp.zeros_like(cross_gate), grad_gate_heads, seq_index * heads, 0
        )
        mod_grad = jnp.concatenate([grad_scale_attn, grad_gate_attn, grad_scale_ffn, grad_gate_ffn])
        mod_total, totals = lax.psum((mod_grad, sums), "seq")
        mod_columns = modulator.shape[1]
        mod_mine = lax.dynamic_slice_in_dim(mod_total, seq_index * mod_columns, mod_columns, 0)
        mod_mine = lax.all_gather(mod_mine.astype(bf16)[None, :], "fsdp", axis=0, tiled=True)
        modulator_grad = dot_tn(cond_mine, mod_mine)
        residual_rms = jnp.sqrt(totals / (length.astype(f32) * width))[:, None]
        small = lax.psum(
            (grad_attn_gain, grad_ffn_gain, grad_query_gain, grad_key_gain, gate_heads_full),
            ("fsdp", "seq"),
        )
        return (
            result.astype(bf16),
            token_grad,
            modulator_grad,
            attn_grads[:, :columns],
            attn_grads[:, columns : 2 * columns],
            attn_grads[:, 2 * columns : 3 * columns],
            attn_grads[:, 3 * columns :].T,
            text_grads[:, :columns],
            text_grads[:, columns:],
            ffn_grads[:, :units],
            ffn_grads[:, units : 2 * units],
            ffn_grads[:, 2 * units :].T,
            small[0],
            small[1],
            small[2],
            small[3],
            small[4],
            residual_rms,
        )

    return local


def solution(mesh):
    by_both = P(("fsdp", "seq"), None)
    return jax.shard_map(
        build(mesh.shape["fsdp"], mesh.shape["seq"]),
        mesh=mesh,
        in_specs=(
            by_both,
            by_both,
            P("fsdp", None),
            P("fsdp", None),
            P(None, "fsdp"),
            P("fsdp"),
            P("fsdp"),
            P("fsdp", "seq"),
            P("fsdp", "seq"),
            P("fsdp", "seq"),
            P("fsdp", "seq"),
            P("seq", "fsdp"),
            P("fsdp", "seq"),
            P("fsdp", "seq"),
            P("fsdp", "seq"),
            P("fsdp", "seq"),
            P("seq", "fsdp"),
            P(),
            P(),
            P(),
            P(),
            P(),
        ),
        out_specs=(
            by_both,
            by_both,
            P("fsdp", "seq"),
            P("fsdp", "seq"),
            P("fsdp", "seq"),
            P("fsdp", "seq"),
            P("seq", "fsdp"),
            P("fsdp", "seq"),
            P("fsdp", "seq"),
            P("fsdp", "seq"),
            P("fsdp", "seq"),
            P("seq", "fsdp"),
            P(),
            P(),
            P(),
            P(),
            P(),
            P(None, "fsdp"),
        ),
        check_vma=False,
    )
```

```python
import math

import jax
import jax.numpy as jnp
from jax import lax
from jax.experimental import pallas as pl
from jax.experimental.pallas import tpu as pltpu
from jax.sharding import PartitionSpec as P

epsilon = 1e-06
masked_score = -1e30
f32 = jnp.float32
bf16 = jnp.bfloat16


def rope_tables(positions, head_size):
    half = head_size // 2
    pair_index = jnp.arange(half)
    frequency = jnp.exp(pair_index.astype(f32) * (-2.0 * math.log(10000.0) / head_size))
    angle = jnp.zeros((positions.shape[1], half), f32)
    for axis_number in range(3):
        chosen = jnp.where(pair_index % 3 == axis_number, frequency, jnp.zeros_like(frequency))
        angle = angle + positions[axis_number].astype(f32)[:, None] * chosen[None, :]
    return (jnp.cos(angle), jnp.sin(angle))


def dot(left, right):
    return jnp.dot(left, right, preferred_element_type=f32)


def dot_nt(left, right):
    return lax.dot_general(left, right, (((1,), (1,)), ((), ())), preferred_element_type=f32)


def dot_tn(left, right):
    return lax.dot_general(left, right, (((0,), (0,)), ((), ())), preferred_element_type=f32)


def attention_forward(qkv, text, cosine, sine, gains, mask, text_mask, gate, heads, head):
    rows = qkv.shape[0]
    columns = heads * head
    block = min(rows, 256)

    def kernel(qkv_ref, text_ref, cos_ref, sin_ref, gain_ref, mask_ref, tmask_ref, gate_ref,
               q_ref, k_ref, v_ref, mixed_ref, cross_ref, lse_ref):
        cos = cos_ref[...]
        sin = sin_ref[...]
        lse_ref[...] = jnp.zeros_like(lse_ref)

        def turned(raw, gain):
            inverse = lax.rsqrt(jnp.mean(raw * raw, axis=-1, keepdims=True) + epsilon)
            value = raw * inverse * gain
            swapped = jnp.concatenate([value[:, head // 2 :], value[:, : head // 2]], axis=1)
            return (value * cos + swapped * sin).astype(bf16)

        for h in range(heads):
            at = slice(h * head, (h + 1) * head)
            q_ref[:, at] = turned(qkv_ref[:, at], gain_ref[0:1, :head])
            k_ref[:, at] = turned(
                qkv_ref[:, columns + h * head : columns + (h + 1) * head], gain_ref[1:2, :head]
            )
            v_ref[:, at] = qkv_ref[:, 2 * columns + h * head : 2 * columns + (h + 1) * head].astype(bf16)

        def attend(query, keys, values, masks):
            scores = dot_nt(query, keys) + masks
            peak = jnp.max(scores, axis=-1, keepdims=True)
            expo = jnp.exp(scores - peak)
            total = jnp.sum(expo, axis=-1, keepdims=True)
            return dot(expo.astype(bf16), values) / total, peak + jnp.log(total)

        for h in range(heads):
            at = slice(h * head, (h + 1) * head)
            keys = k_ref[:, at]
            values = v_ref[:, at]
            text_keys = text_ref[:, at]
            text_values = text_ref[:, columns + h * head : columns + (h + 1) * head]
            for b in range(rows // block):
                here = slice(b * block, (b + 1) * block)
                query = q_ref[here, at] * jnp.asarray(head**-0.5, bf16)
                own, own_lse = attend(query, keys, values, mask_ref[...])
                other, other_lse = attend(query, text_keys, text_values, tmask_ref[...])
                cross_ref[here, at] = other
                mixed_ref[here, at] = (own + gate_ref[:, at] * other).astype(bf16)
                lse_ref[here, h : h + 1] = own_lse
                lse_ref[here, heads + h : heads + h + 1] = other_lse

    wide = jax.ShapeDtypeStruct((rows, columns), bf16)
    return pl.pallas_call(
        kernel,
        out_shape=(wide, wide, wide, wide, jax.ShapeDtypeStruct((rows, columns), f32),
                   jax.ShapeDtypeStruct((rows, 128), f32)),
        in_specs=[pl.BlockSpec(memory_space=pltpu.VMEM)] * 8,
        out_specs=(pl.BlockSpec(memory_space=pltpu.VMEM),) * 6,
        compiler_params=pltpu.CompilerParams(vmem_limit_bytes=48 * 1024 * 1024),
        cost_estimate=pl.CostEstimate(
            flops=4 * rows * (rows + text.shape[0]) * columns,
            bytes_accessed=8 * rows * columns * 4,
            transcendentals=heads * rows * (rows + text.shape[0]),
        ),
        name="attention_forward",
    )(qkv, text, cosine, sine, gains, mask, text_mask, gate)


def attention_backward(qkv, query, key, value, text, grad, lse, cross, cosine, sine, gains, mask, text_mask, gate, heads, head):
    rows = qkv.shape[0]
    text_rows = text.shape[0]
    columns = heads * head
    block = min(rows, 256)
    scale = head**-0.5

    def kernel(qkv_ref, q_ref, k_ref, v_ref, text_ref, grad_ref, lse_ref, cross_ref, cos_ref, sin_ref,
               gain_ref, mask_ref, tmask_ref, gate_ref, rows_ref, text_rows_ref, small_ref,
               dq_ref, dk_ref, dv_ref, dtk_ref, dtv_ref):
        cos = cos_ref[...]
        sin = sin_ref[...]
        small_ref[...] = jnp.zeros_like(small_ref)

        def soft_back(query, keys, values, masks, lse, back):
            probs = jnp.exp(dot_nt(query, keys) + masks - lse)
            grad_probs = dot_nt(back, values)
            delta = jnp.sum(probs * grad_probs, axis=-1, keepdims=True)
            return probs.astype(bf16), (probs * (grad_probs - delta)).astype(bf16)

        def raw_back(grad, raw, gain, row):
            swapped = jnp.concatenate([grad[:, head // 2 :], grad[:, : head // 2]], axis=1)
            turned = grad * cos - swapped * sin
            inverse = lax.rsqrt(jnp.mean(raw * raw, axis=-1, keepdims=True) + epsilon)
            unit = raw * inverse
            small_ref[row : row + 1, :head] += jnp.sum(turned * unit, axis=0, keepdims=True)
            scaled = turned * gain
            return (
                inverse * (scaled - unit * jnp.mean(scaled * unit, axis=-1, keepdims=True))
            ).astype(bf16)

        for h in range(heads):
            at = slice(h * head, (h + 1) * head)
            at_key = slice(columns + h * head, columns + (h + 1) * head)
            at_value = slice(2 * columns + h * head, 2 * columns + (h + 1) * head)
            keys = k_ref[:, at]
            values = v_ref[:, at]
            text_keys = text_ref[:, at]
            text_values = text_ref[:, at_key]
            gate_row = gate_ref[:, at]
            for b in range(rows // block):
                here = slice(b * block, (b + 1) * block)
                plain = q_ref[here, at]
                query = plain * jnp.asarray(scale, bf16)
                back = grad_ref[here, at]
                wide = back.astype(f32)
                probs, grads = soft_back(query, keys, values, mask_ref[...], lse_ref[here, h : h + 1], back)
                dq = dot(grads, keys)
                dk = dot_tn(grads, query)
                dv = dot_tn(probs, back)
                cross_back = (wide * gate_row).astype(bf16)
                probs, grads = soft_back(
                    query, text_keys, text_values, tmask_ref[...],
                    lse_ref[here, heads + h : heads + h + 1], cross_back,
                )
                dq_ref[here, :] = (dq + dot(grads, text_keys)) * scale
                dtk = dot_tn(grads, query)
                dtv = dot_tn(probs, cross_back)
                small_ref[2:3, h * head : (h + 1) * head] += jnp.sum(
                    wide * cross_ref[here, at], axis=0, keepdims=True
                )
                if b == 0:
                    dk_ref[...] = dk
                    dv_ref[...] = dv
                    dtk_ref[...] = dtk
                    dtv_ref[...] = dtv
                else:
                    dk_ref[...] += dk
                    dv_ref[...] += dv
                    dtk_ref[...] += dtk
                    dtv_ref[...] += dtv
            rows_ref[:, at] = raw_back(dq_ref[...], qkv_ref[:, at], gain_ref[0:1, :head], 0)
            rows_ref[:, at_key] = raw_back(dk_ref[...], qkv_ref[:, at_key], gain_ref[1:2, :head], 1)
            rows_ref[:, at_value] = dv_ref[...].astype(bf16)
            text_rows_ref[:, at] = dtk_ref[...].astype(bf16)
            text_rows_ref[:, at_key] = dtv_ref[...].astype(bf16)

    return pl.pallas_call(
        kernel,
        out_shape=(
            jax.ShapeDtypeStruct((rows, 3 * columns), bf16),
            jax.ShapeDtypeStruct((text_rows, 2 * columns), bf16),
            jax.ShapeDtypeStruct((8, max(columns, 128)), f32),
        ),
        in_specs=[pl.BlockSpec(memory_space=pltpu.VMEM)] * 14,
        out_specs=(pl.BlockSpec(memory_space=pltpu.VMEM),) * 3,
        scratch_shapes=[pltpu.VMEM((rows, head), f32)] * 3 + [pltpu.VMEM((text_rows, head), f32)] * 2,
        compiler_params=pltpu.CompilerParams(vmem_limit_bytes=48 * 1024 * 1024),
        cost_estimate=pl.CostEstimate(
            flops=10 * rows * (rows + text_rows) * columns,
            bytes_accessed=12 * rows * columns * 4,
            transcendentals=heads * rows * (rows + text_rows),
        ),
        name="attention_backward",
    )(qkv, query, key, value, text, grad, lse, cross, cosine, sine, gains, mask, text_mask, gate)


def ffn_forward(ffn_in, weights):
    rows, width = ffn_in.shape
    units = weights.shape[1] // 2
    tile = min(units, 256)
    tiles = units // tile

    def kernel(in_ref, gate_ref, up_ref, hidden_ref, by_gate_ref, by_up_ref):
        gate_act = dot(in_ref[...], gate_ref[...])
        up_act = dot(in_ref[...], up_ref[...])
        sigmoid = 1.0 / (1.0 + jnp.exp(-gate_act))
        silu = gate_act * sigmoid
        hidden_ref[...] = (silu * up_act).astype(bf16)
        by_gate_ref[...] = up_act * sigmoid * (1.0 + gate_act * (1.0 - sigmoid))
        by_up_ref[...] = silu

    part = pl.BlockSpec((rows, tile), lambda j: (0, j))
    wide = jax.ShapeDtypeStruct((rows, units), f32)
    return pl.pallas_call(
        kernel,
        grid=(tiles,),
        out_shape=(jax.ShapeDtypeStruct((rows, units), bf16), wide, wide),
        in_specs=[
            pl.BlockSpec((rows, width), lambda j: (0, 0)),
            pl.BlockSpec((width, tile), lambda j: (0, j)),
            pl.BlockSpec((width, tile), lambda j: (0, tiles + j)),
        ],
        out_specs=(part, part, part),
        compiler_params=pltpu.CompilerParams(vmem_limit_bytes=48 * 1024 * 1024),
        cost_estimate=pl.CostEstimate(
            flops=4 * rows * width * units,
            bytes_accessed=2 * rows * width + 4 * width * units + 10 * rows * units,
            transcendentals=rows * units,
        ),
        name="ffn_forward",
    )(ffn_in, weights, weights)


def ffn_backward(back, down, weights, by_gate, by_up):
    rows, width = back.shape
    units = down.shape[1]
    tile = min(units, 256)
    tiles = units // tile

    def kernel(back_ref, down_ref, gate_ref, up_ref, by_gate_ref, by_up_ref, act_ref, grad_ref, total):
        step = pl.program_id(0)

        @pl.when(step == 0)
        def _():
            total[...] = jnp.zeros_like(total)

        grad_hidden = dot(back_ref[...], down_ref[...])
        grad_gate = (grad_hidden * by_gate_ref[...]).astype(bf16)
        grad_up = (grad_hidden * by_up_ref[...]).astype(bf16)
        act_ref[:, pl.ds(pl.multiple_of(step * tile, tile), tile)] = grad_gate
        act_ref[:, pl.ds(pl.multiple_of(units + step * tile, tile), tile)] = grad_up
        total[...] += dot_nt(grad_gate, gate_ref[...]) + dot_nt(grad_up, up_ref[...])

        @pl.when(step == tiles - 1)
        def _():
            grad_ref[...] = total[...].astype(bf16)

    whole = pl.BlockSpec((rows, width), lambda j: (0, 0))
    part = pl.BlockSpec((rows, tile), lambda j: (0, j))
    return pl.pallas_call(
        kernel,
        grid=(tiles,),
        out_shape=(
            jax.ShapeDtypeStruct((rows, 2 * units), bf16),
            jax.ShapeDtypeStruct((rows, width), bf16),
        ),
        in_specs=[
            whole,
            pl.BlockSpec((width, tile), lambda j: (0, j)),
            pl.BlockSpec((width, tile), lambda j: (0, j)),
            pl.BlockSpec((width, tile), lambda j: (0, tiles + j)),
            part,
            part,
        ],
        out_specs=(pl.BlockSpec((rows, 2 * units), lambda j: (0, 0)), whole),
        scratch_shapes=[pltpu.VMEM((rows, width), f32)],
        compiler_params=pltpu.CompilerParams(vmem_limit_bytes=48 * 1024 * 1024),
        cost_estimate=pl.CostEstimate(
            flops=6 * rows * width * units,
            bytes_accessed=6 * rows * width + 6 * width * units + 12 * rows * units,
            transcendentals=0,
        ),
        name="ffn_backward",
    )(back, down, weights, weights, by_gate, by_up)


def widen(block, parts):
    rows = block.shape[0]
    columns = block.shape[1] // parts

    def kernel(block_ref, *part_refs):
        for i, part_ref in enumerate(part_refs):
            part_ref[...] = block_ref[:, i * columns : (i + 1) * columns].astype(f32)

    return pl.pallas_call(
        kernel,
        out_shape=[jax.ShapeDtypeStruct((rows, columns), f32)] * parts,
        in_specs=[pl.BlockSpec(memory_space=pltpu.VMEM)],
        out_specs=[pl.BlockSpec(memory_space=pltpu.VMEM)] * parts,
        name="widen",
    )(block)


def build(n_f, n_s):
    n_z = n_f // 2
    swaps = [[(i, i ^ k) for i in range(n_s)] for k in range(n_s)]

    def twin(block):
        return lax.ppermute(block, "fsdp", [(i, i ^ 1) for i in range(n_f)])

    def fsdp_xor(block, k):
        return lax.ppermute(block, "fsdp", [(i, i ^ k) for i in range(n_f)])

    def after(block, *earlier):
        return lax.optimization_barrier((block,) + earlier)[0]

    def stage(*values):
        return lax.optimization_barrier(values)

    def fsdp_scatter(total):
        return lax.psum_scatter(total, "fsdp", scatter_dimension=0, tiled=True)

    class Gather:
        def __init__(self, own, core):
            got = twin(own)
            first = core == 0
            pair = [jnp.where(first, own, got), jnp.where(first, got, own)]
            self.got = [jnp.concatenate(pair, axis=0)]
            self.twins = [None]

        def step(self, last=None):
            last = n_z - 1 if last is None else last
            while len(self.got) <= last:
                k = len(self.got)
                pairs = [(2 * z, 2 * z + 2) for z in range(k - 1, n_z - 1)]
                pairs += [(2 * z + 1, 2 * z - 1) for z in range(1, n_z - k + 1)]
                self.got.append(lax.ppermute(self.got[-1], "fsdp", pairs))

        def pass_on(self, last=None):
            last = n_z - 1 if last is None else last
            while len(self.twins) <= last:
                self.twins.append(twin(self.got[len(self.twins)]))

        def full(self, chip, core, place):
            rows, columns = self.got[0].shape
            whole = jnp.zeros((n_z, rows, columns), self.got[0].dtype)
            for k in range(n_z):
                block = self.got[0] if k == 0 else self.got[k] + self.twins[n_z - k]
                at = jnp.where(core == 0, lax.rem(chip + n_z - k, n_z), lax.rem(chip + k, n_z))
                whole = lax.dynamic_update_slice(whole, block[None], (place(at), 0, 0))
            return whole.reshape(n_z * rows, columns)

    def seq_near(block):
        return [lax.ppermute(block, "seq", swaps[k]) for k in (1, 2)]

    def seq_far(near, axis=0):
        half = near[0].shape[axis] // 2
        return [
            lax.ppermute(lax.slice_in_dim(near[0], 0, half, axis=axis), "seq", swaps[2]),
            lax.ppermute(lax.slice_in_dim(near[1], half, 2 * half, axis=axis), "seq", swaps[1]),
        ]

    def seq_gather(block, axis=0):
        if n_s != 4:
            parts = [block] + [lax.ppermute(block, "seq", swaps[k]) for k in range(1, n_s)]
        else:
            near = seq_near(block)
            far = jnp.concatenate(seq_far(near, axis + 1 if axis else 0), axis=axis + 1) if axis else None
            parts = [block] + near + ([far] if axis else seq_far(near))
        return jnp.concatenate(parts, axis=axis)

    def seq_send(total, rows):
        return [
            lax.ppermute(total[k * rows : (k + 1) * rows].astype(bf16), "seq", swaps[k])
            for k in range(1, n_s)
        ]

    def seq_sum(total, parts, rows):
        result = total[:rows].astype(f32)
        for part in parts:
            result = result + part.astype(f32)
        return result

    def by_seq(stacked, index):
        bit = 1
        while bit < n_s:
            split = stacked.reshape((n_s // (2 * bit), 2, bit) + stacked.shape[1:])
            turn = (index & bit) != 0
            first = jnp.where(turn, split[:, 1], split[:, 0])
            second = jnp.where(turn, split[:, 0], split[:, 1])
            stacked = jnp.stack([first, second], axis=1).reshape(stacked.shape)
            bit *= 2
        return stacked

    def all_sum(block, axis, size):
        bit = 1
        while bit < size:
            block = block + lax.ppermute(block, axis, [(i, i ^ bit) for i in range(size)])
            bit *= 2
        return block

    def local(
        tokens,
        cotangent,
        condition,
        caption,
        positions,
        clip_lengths,
        caption_lengths,
        modulator,
        query_weight,
        key_weight,
        value_weight,
        output_weight,
        textkey_weight,
        textvalue_weight,
        gate_weight,
        up_weight,
        down_weight,
        attn_gain,
        ffn_gain,
        query_gain,
        key_gain,
        cross_gate,
    ):
        rows = tokens.shape[0]
        width = tokens.shape[1]
        head_size = query_gain.shape[0]
        columns = query_weight.shape[1]
        heads = columns // head_size
        units = gate_weight.shape[1]
        clip_rows = positions.shape[1]
        text_rows = caption.shape[0]
        seq_index = lax.axis_index("seq")
        fsdp_index = lax.axis_index("fsdp")
        length = clip_lengths[0]
        text_length = caption_lengths[0]
        scale = head_size ** (-0.5)

        chip = fsdp_index // 2
        core = fsdp_index % 2

        def straight(t):
            return t

        def turned(t):
            return t ^ chip

        def fsdp_gather(*parts):
            return lax.all_gather(jnp.concatenate(parts, axis=1), "fsdp", axis=0, tiled=True)

        attn_full = fsdp_gather(query_weight, key_weight, value_weight, output_weight.T)
        text_full = fsdp_gather(textkey_weight, textvalue_weight)
        ffn_full = fsdp_gather(gate_weight, up_weight)
        down_t = lax.all_gather(down_weight.T, "fsdp", axis=0, tiled=True)
        qkv_full = attn_full[:, : 3 * columns]
        output_t = attn_full[:, 3 * columns :]
        cap_rows = text_rows // n_s
        cap_columns = textkey_weight.shape[0]
        cap_piece = lax.dynamic_slice_in_dim(caption, seq_index * cap_rows, cap_rows, 0)
        cap_mine = jnp.stack(
            [
                lax.dynamic_slice_in_dim(cap_piece, (fsdp_index ^ k) * cap_columns, cap_columns, 1)
                for k in range(n_f)
            ]
        )
        bit = 1
        while bit < n_f:
            split = cap_mine.reshape(n_f // (2 * bit), 2, bit, cap_rows, cap_columns)
            got = fsdp_xor(split[:, 1], bit)
            cap_mine = jnp.stack([split[:, 0], got], axis=1).reshape(n_f, cap_rows, cap_columns)
            bit *= 2
        cap_mine = cap_mine.reshape(n_z, 2, cap_rows, cap_columns)
        cap_mine = jnp.stack(
            [
                jnp.where(core == 0, cap_mine[:, 0], cap_mine[:, 1]),
                jnp.where(core == 0, cap_mine[:, 1], cap_mine[:, 0]),
            ],
            axis=1,
        )
        cap_mine = cap_mine.reshape(n_f, cap_rows, cap_columns)
        cond_low = jax.nn.silu(condition.astype(f32)).astype(bf16)
        cond_all = cond_low
        bit = 1
        while bit < n_f:
            cond_all = jnp.concatenate([cond_all, fsdp_xor(cond_all, bit)], axis=0)
            bit *= 2
        tokens_all = seq_gather(tokens)
        cond_all, cap_mine, tokens_all = stage(cond_all, cap_mine, tokens_all)

        mod_rows = modulator.shape[0]
        cond_mine = lax.dynamic_slice_in_dim(cond_all, fsdp_index * mod_rows, mod_rows, 1)
        mod_part = dot(cond_mine, modulator)
        half = n_f // 2
        while half:
            mod_part = mod_part[:half] + fsdp_xor(mod_part[half:], half)
            half //= 2
        cap_all = seq_gather(cap_mine[:, None], 1)
        modulation = mod_part
        bit = 1
        while bit < n_s:
            modulation = jnp.concatenate(
                [modulation, lax.ppermute(modulation, "seq", swaps[bit])], axis=0
            )
            bit *= 2
        modulation = by_seq(modulation, seq_index).reshape(-1)
        modulation, cap_all = stage(modulation, cap_all)
        cap_all = cap_all.reshape(n_f * text_rows, cap_columns)
        tokens_all = tokens_all.astype(f32)
        cotangent_all = seq_gather(after(cotangent, cap_all)).astype(f32)

        scale_attn = modulation[:width]
        gate_attn = modulation[width : 2 * width]
        scale_ffn = modulation[2 * width : 3 * width]
        gate_ffn = modulation[3 * width :]
        tanh_attn = jnp.tanh(gate_attn)
        tanh_ffn = jnp.tanh(gate_ffn)

        order = [seq_index ^ k for k in range(n_s)]
        row_index = jnp.concatenate([order[k] * rows + jnp.arange(rows) for k in range(n_s)])
        places = jnp.concatenate(
            [lax.dynamic_slice_in_dim(positions, order[k] * rows, rows, 1) for k in range(n_s)],
            axis=1,
        )

        inv_attn_all = lax.rsqrt(jnp.mean(tokens_all * tokens_all, axis=-1, keepdims=True) + epsilon)
        normed_all = (tokens_all * inv_attn_all * attn_gain * (1.0 + scale_attn)).astype(bf16)
        inputs = tokens.astype(f32)
        inv_attn = inv_attn_all[:rows]
        unit_attn = inputs * inv_attn
        qkv = dot(normed_all, qkv_full)
        text_both = dot(caption, text_full).astype(bf16)
        cosine, sine = rope_tables(places, head_size)
        cosine = jnp.concatenate([cosine, cosine], axis=1)
        sine = jnp.concatenate([-sine, sine], axis=1)
        gains = jnp.zeros((8, head_size), f32).at[0].set(query_gain).at[1].set(key_gain)
        mask = jnp.where(row_index < length, 0.0, masked_score).astype(f32)[None, :]
        text_mask = jnp.where(jnp.arange(text_rows) < text_length, 0.0, masked_score).astype(f32)[None, :]
        gate_heads = jnp.tanh(lax.dynamic_slice_in_dim(cross_gate, seq_index * heads, heads))
        gate_row = jnp.repeat(gate_heads, head_size)[None, :]
        query_rot, key_rot, value_low, mixed_rows, cross_out, lse = attention_forward(
            qkv, text_both, cosine, sine, gains, mask, text_mask, gate_row, heads, head_size
        )
        attn_sent = dot_nt(mixed_rows, output_t)
        attn_out = seq_sum(attn_sent, seq_send(attn_sent, rows), rows)
        branch_attn = tanh_attn * attn_out
        hidden_in = inputs + branch_attn
        inv_ffn = lax.rsqrt(jnp.mean(hidden_in * hidden_in, axis=-1, keepdims=True) + epsilon)
        unit_ffn = hidden_in * inv_ffn
        ffn_in = (unit_ffn * ffn_gain * (1.0 + scale_ffn)).astype(bf16)
        ffn_all = seq_gather(ffn_in)
        ffn_back_all = (tanh_ffn * cotangent_all).astype(bf16)
        hidden, by_gate, by_up = ffn_forward(ffn_all, ffn_full)
        down_part = dot_tn(ffn_back_all, hidden).astype(bf16)
        down_grads = fsdp_scatter(down_part)
        grad_act, grad_sent = ffn_backward(
            ffn_back_all, after(down_t, down_part), ffn_full, by_gate, by_up
        )
        parts = seq_send(grad_sent, rows)
        act_part = dot_tn(ffn_all, grad_act).astype(bf16)
        act_grads = fsdp_scatter(act_part)
        parts[0] = after(parts[0], act_part)
        grad_ffn_in = seq_sum(grad_sent, parts, rows)
        grad_out = cotangent.astype(f32)
        grad_ffn_gain = jnp.sum(grad_ffn_in * unit_ffn * (1.0 + scale_ffn), axis=0)
        grad_scale_ffn = jnp.sum(grad_ffn_in * unit_ffn * ffn_gain, axis=0)
        scaled_ffn = grad_ffn_in * ffn_gain * (1.0 + scale_ffn)
        grad_hidden_in = grad_out + inv_ffn * (
            scaled_ffn - unit_ffn * jnp.mean(scaled_ffn * unit_ffn, axis=-1, keepdims=True)
        )
        attn_back = (tanh_attn * grad_hidden_in).astype(bf16)
        grad_gate_attn = jnp.sum(grad_hidden_in * attn_out, axis=0) * (1.0 - tanh_attn * tanh_attn)
        attn_back_all = seq_gather(attn_back)
        grad_mixed = dot(attn_back_all, output_t).astype(bf16)
        output_part = dot_tn(attn_back_all, mixed_rows).astype(bf16)
        ffn_sent = dot_nt(after(hidden, attn_back_all), down_t)
        ffn_parts = seq_send(ffn_sent, rows)
        qkv_rows, text_grads_rows, head_sums = attention_backward(
            qkv, query_rot, key_rot, value_low, text_both, grad_mixed, lse, cross_out,
            cosine, sine, gains, mask, text_mask, gate_row, heads, head_size,
        )
        qkv_rows, text_grads_rows, *ffn_parts = stage(qkv_rows, text_grads_rows, *ffn_parts)

        text_order = [
            lax.dynamic_slice_in_dim(text_grads_rows, order[k] * cap_rows, cap_rows, 0)
            for k in range(n_s)
        ]
        text_back = Gather(jnp.concatenate(text_order, axis=0), core)
        text_back.step(1)
        normed_sent = dot_nt(qkv_rows, qkv_full)
        parts = seq_send(normed_sent, rows)
        qkv_part = dot_tn(normed_all, after(qkv_rows, normed_sent)).astype(bf16)
        attn_part = jnp.concatenate([qkv_part, output_part], axis=1)
        ffn_out = seq_sum(ffn_sent, ffn_parts, rows)
        branch_ffn = tanh_ffn * ffn_out
        result = hidden_in + branch_ffn
        row_valid = (seq_index * rows + jnp.arange(rows) < length)[:, None]
        sums = jnp.stack(
            [
                jnp.sum(jnp.where(row_valid, result * result, 0.0)),
                jnp.sum(jnp.where(row_valid, branch_attn * branch_attn, 0.0)),
                jnp.sum(jnp.where(row_valid, branch_ffn * branch_ffn, 0.0)),
            ]
        )
        grad_gate_ffn = jnp.sum(grad_out * ffn_out, axis=0) * (1.0 - tanh_ffn * tanh_ffn)

        grad_query_gain = head_sums[0, :head_size]
        grad_key_gain = head_sums[1, :head_size]
        grad_gate_heads = jnp.sum(
            head_sums[2, :columns].reshape(heads, head_size), axis=1
        ) * (1.0 - gate_heads * gate_heads)
        attn_grads = fsdp_scatter(after(attn_part, act_grads))
        *parts, text_back.got[1] = stage(*parts, text_back.got[1])

        text_back.step(2)
        text_back.pass_on(1)
        grad_normed = seq_sum(normed_sent, parts, rows)
        grad_attn_gain = jnp.sum(grad_normed * unit_attn * (1.0 + scale_attn), axis=0)
        grad_scale_attn = jnp.sum(grad_normed * unit_attn * attn_gain, axis=0)
        scaled_attn = grad_normed * attn_gain * (1.0 + scale_attn)
        token_grad = grad_hidden_in + inv_attn * (
            scaled_attn - unit_attn * jnp.mean(scaled_attn * unit_attn, axis=-1, keepdims=True)
        )

        gate_heads_full = lax.dynamic_update_slice_in_dim(
            jnp.zeros_like(cross_gate), grad_gate_heads, seq_index * heads, 0
        )
        sizes = jnp.concatenate(
            [grad_attn_gain, grad_ffn_gain, gate_heads_full, grad_query_gain, grad_key_gain, sums]
        )
        sizes = all_sum(sizes, "seq", n_s)
        mod_grad = jnp.concatenate([grad_scale_attn, grad_gate_attn, grad_scale_ffn, grad_gate_ffn])
        mod_mine = by_seq(mod_grad.reshape(n_s, -1), seq_index)
        half = n_s // 2
        while half:
            mod_mine = mod_mine[:half] + lax.ppermute(mod_mine[half:], "seq", swaps[half])
            half //= 2
        mod_mine = mod_mine.astype(bf16)
        sizes, mod_mine, text_back.got[2] = stage(sizes, mod_mine, text_back.got[2])

        text_back.step()
        text_back.pass_on(2)
        bit = 1
        while bit < n_f:
            mod_mine = jnp.concatenate([mod_mine, fsdp_xor(mod_mine, bit)], axis=0)
            bit *= 2
        modulator_grad = dot_tn(cond_mine, mod_mine)
        totals = sizes[-3:]
        residual_rms = jnp.sqrt(totals / (length.astype(f32) * width))[:, None]
        small = all_sum(sizes[:-3], "fsdp", n_f)
        small, modulator_grad, text_back.got[-1] = stage(
            small, modulator_grad, text_back.got[-1]
        )

        text_back.pass_on()
        text_grads = dot_tn(cap_all, text_back.full(chip, core, turned))
        attn_grads = widen(attn_grads, 4)
        act_grads = widen(act_grads, 2)
        down_grads = widen(down_grads, 1)[0]
        n_heads = cross_gate.shape[0]
        ends = [width, width, n_heads, head_size, head_size]
        ends = [sum(ends[:i]) for i in range(6)]
        small = [small[ends[i] : ends[i + 1]] for i in range(5)]
        small = (small[0], small[1], small[3], small[4], small[2])
        return (
            result.astype(bf16),
            token_grad,
            modulator_grad,
            *attn_grads[:3],
            attn_grads[3].T,
            text_grads[:, :columns],
            text_grads[:, columns:],
            *act_grads,
            down_grads.T,
            small[0],
            small[1],
            small[2],
            small[3],
            small[4],
            residual_rms,
        )

    return local


def solution(mesh):
    by_both = P(("fsdp", "seq"), None)
    return jax.shard_map(
        build(mesh.shape["fsdp"], mesh.shape["seq"]),
        mesh=mesh,
        in_specs=(
            by_both,
            by_both,
            P("fsdp", None),
            P("fsdp", None),
            P(None, "fsdp"),
            P("fsdp"),
            P("fsdp"),
            P("fsdp", "seq"),
            P("fsdp", "seq"),
            P("fsdp", "seq"),
            P("fsdp", "seq"),
            P("seq", "fsdp"),
            P("fsdp", "seq"),
            P("fsdp", "seq"),
            P("fsdp", "seq"),
            P("fsdp", "seq"),
            P("seq", "fsdp"),
            P(),
            P(),
            P(),
            P(),
            P(),
        ),
        out_specs=(
            by_both,
            by_both,
            P("fsdp", "seq"),
            P("fsdp", "seq"),
            P("fsdp", "seq"),
            P("fsdp", "seq"),
            P("seq", "fsdp"),
            P("fsdp", "seq"),
            P("fsdp", "seq"),
            P("fsdp", "seq"),
            P("fsdp", "seq"),
            P("seq", "fsdp"),
            P(),
            P(),
            P(),
            P(),
            P(),
            P(None, "fsdp"),
        ),
        check_vma=False,
    )
```

```python
import math

import jax
import jax.numpy as jnp
from jax import lax
from jax.experimental import pallas as pl
from jax.experimental.pallas import tpu as pltpu
from jax.sharding import PartitionSpec as P

epsilon = 1e-06
masked_score = -1e30
f32 = jnp.float32
bf16 = jnp.bfloat16


def rope_tables(positions, head_size):
    half = head_size // 2
    pair_index = jnp.arange(half)
    frequency = jnp.exp(pair_index.astype(f32) * (-2.0 * math.log(10000.0) / head_size))
    angle = jnp.zeros((positions.shape[1], half), f32)
    for axis_number in range(3):
        chosen = jnp.where(pair_index % 3 == axis_number, frequency, jnp.zeros_like(frequency))
        angle = angle + positions[axis_number].astype(f32)[:, None] * chosen[None, :]
    return (jnp.cos(angle), jnp.sin(angle))


def dot(left, right):
    return jnp.dot(left, right, preferred_element_type=f32)


def dot_nt(left, right):
    return lax.dot_general(left, right, (((1,), (1,)), ((), ())), preferred_element_type=f32)


def dot_tn(left, right):
    return lax.dot_general(left, right, (((0,), (0,)), ((), ())), preferred_element_type=f32)


def attention_forward(qkv, text, cosine, sine, gains, mask, text_mask, gate, heads, head):
    rows = qkv.shape[0]
    columns = heads * head
    block = min(rows, 256)

    def kernel(qkv_ref, text_ref, cos_ref, sin_ref, gain_ref, mask_ref, tmask_ref, gate_ref,
               q_ref, k_ref, v_ref, mixed_ref, cross_ref, lse_ref):
        cos = cos_ref[...]
        sin = sin_ref[...]
        lse_ref[...] = jnp.zeros_like(lse_ref)

        def turned(raw, gain):
            inverse = lax.rsqrt(jnp.mean(raw * raw, axis=-1, keepdims=True) + epsilon)
            value = raw * inverse * gain
            swapped = jnp.concatenate([value[:, head // 2 :], value[:, : head // 2]], axis=1)
            return (value * cos + swapped * sin).astype(bf16)

        for h in range(heads):
            at = slice(h * head, (h + 1) * head)
            q_ref[:, at] = turned(qkv_ref[:, at], gain_ref[0:1, :head])
            k_ref[:, at] = turned(
                qkv_ref[:, columns + h * head : columns + (h + 1) * head], gain_ref[1:2, :head]
            )
            v_ref[:, at] = qkv_ref[:, 2 * columns + h * head : 2 * columns + (h + 1) * head].astype(bf16)

        def attend(query, keys, values, masks):
            scores = dot_nt(query, keys) + masks
            peak = jnp.max(scores, axis=-1, keepdims=True)
            expo = jnp.exp(scores - peak)
            total = jnp.sum(expo, axis=-1, keepdims=True)
            return dot(expo.astype(bf16), values) / total, peak + jnp.log(total)

        for h in range(heads):
            at = slice(h * head, (h + 1) * head)
            keys = k_ref[:, at]
            values = v_ref[:, at]
            text_keys = text_ref[:, at]
            text_values = text_ref[:, columns + h * head : columns + (h + 1) * head]
            for b in range(rows // block):
                here = slice(b * block, (b + 1) * block)
                query = q_ref[here, at] * jnp.asarray(head**-0.5, bf16)
                own, own_lse = attend(query, keys, values, mask_ref[...])
                other, other_lse = attend(query, text_keys, text_values, tmask_ref[...])
                cross_ref[here, at] = other
                mixed_ref[here, at] = (own + gate_ref[:, at] * other).astype(bf16)
                lse_ref[here, h : h + 1] = own_lse
                lse_ref[here, heads + h : heads + h + 1] = other_lse

    wide = jax.ShapeDtypeStruct((rows, columns), bf16)
    return pl.pallas_call(
        kernel,
        out_shape=(wide, wide, wide, wide, jax.ShapeDtypeStruct((rows, columns), f32),
                   jax.ShapeDtypeStruct((rows, 128), f32)),
        in_specs=[pl.BlockSpec(memory_space=pltpu.VMEM)] * 8,
        out_specs=(pl.BlockSpec(memory_space=pltpu.VMEM),) * 6,
        compiler_params=pltpu.CompilerParams(vmem_limit_bytes=48 * 1024 * 1024),
        cost_estimate=pl.CostEstimate(
            flops=4 * rows * (rows + text.shape[0]) * columns,
            bytes_accessed=8 * rows * columns * 4,
            transcendentals=heads * rows * (rows + text.shape[0]),
        ),
        name="attention_forward",
    )(qkv, text, cosine, sine, gains, mask, text_mask, gate)


def attention_backward(qkv, query, key, value, text, grad, lse, cross, cosine, sine, gains, mask, text_mask, gate, heads, head):
    rows = qkv.shape[0]
    text_rows = text.shape[0]
    columns = heads * head
    block = min(rows, 256)
    scale = head**-0.5

    def kernel(qkv_ref, q_ref, k_ref, v_ref, text_ref, grad_ref, lse_ref, cross_ref, cos_ref, sin_ref,
               gain_ref, mask_ref, tmask_ref, gate_ref, rows_ref, text_rows_ref, small_ref,
               dq_ref, dk_ref, dv_ref, dtk_ref, dtv_ref):
        cos = cos_ref[...]
        sin = sin_ref[...]
        small_ref[...] = jnp.zeros_like(small_ref)

        def soft_back(query, keys, values, masks, lse, back):
            probs = jnp.exp(dot_nt(query, keys) + masks - lse)
            grad_probs = dot_nt(back, values)
            delta = jnp.sum(probs * grad_probs, axis=-1, keepdims=True)
            return probs.astype(bf16), (probs * (grad_probs - delta)).astype(bf16)

        def raw_back(grad, raw, gain, row):
            swapped = jnp.concatenate([grad[:, head // 2 :], grad[:, : head // 2]], axis=1)
            turned = grad * cos - swapped * sin
            inverse = lax.rsqrt(jnp.mean(raw * raw, axis=-1, keepdims=True) + epsilon)
            unit = raw * inverse
            small_ref[row : row + 1, :head] += jnp.sum(turned * unit, axis=0, keepdims=True)
            scaled = turned * gain
            return (
                inverse * (scaled - unit * jnp.mean(scaled * unit, axis=-1, keepdims=True))
            ).astype(bf16)

        for h in range(heads):
            at = slice(h * head, (h + 1) * head)
            at_key = slice(columns + h * head, columns + (h + 1) * head)
            at_value = slice(2 * columns + h * head, 2 * columns + (h + 1) * head)
            keys = k_ref[:, at]
            values = v_ref[:, at]
            text_keys = text_ref[:, at]
            text_values = text_ref[:, at_key]
            gate_row = gate_ref[:, at]
            for b in range(rows // block):
                here = slice(b * block, (b + 1) * block)
                plain = q_ref[here, at]
                query = plain * jnp.asarray(scale, bf16)
                back = grad_ref[here, at]
                wide = back.astype(f32)
                probs, grads = soft_back(query, keys, values, mask_ref[...], lse_ref[here, h : h + 1], back)
                dq = dot(grads, keys)
                dk = dot_tn(grads, query)
                dv = dot_tn(probs, back)
                cross_back = (wide * gate_row).astype(bf16)
                probs, grads = soft_back(
                    query, text_keys, text_values, tmask_ref[...],
                    lse_ref[here, heads + h : heads + h + 1], cross_back,
                )
                dq_ref[here, :] = (dq + dot(grads, text_keys)) * scale
                dtk = dot_tn(grads, query)
                dtv = dot_tn(probs, cross_back)
                small_ref[2:3, h * head : (h + 1) * head] += jnp.sum(
                    wide * cross_ref[here, at], axis=0, keepdims=True
                )
                if b == 0:
                    dk_ref[...] = dk
                    dv_ref[...] = dv
                    dtk_ref[...] = dtk
                    dtv_ref[...] = dtv
                else:
                    dk_ref[...] += dk
                    dv_ref[...] += dv
                    dtk_ref[...] += dtk
                    dtv_ref[...] += dtv
            rows_ref[:, at] = raw_back(dq_ref[...], qkv_ref[:, at], gain_ref[0:1, :head], 0)
            rows_ref[:, at_key] = raw_back(dk_ref[...], qkv_ref[:, at_key], gain_ref[1:2, :head], 1)
            rows_ref[:, at_value] = dv_ref[...].astype(bf16)
            text_rows_ref[:, at] = dtk_ref[...].astype(bf16)
            text_rows_ref[:, at_key] = dtv_ref[...].astype(bf16)

    return pl.pallas_call(
        kernel,
        out_shape=(
            jax.ShapeDtypeStruct((rows, 3 * columns), bf16),
            jax.ShapeDtypeStruct((text_rows, 2 * columns), bf16),
            jax.ShapeDtypeStruct((8, max(columns, 128)), f32),
        ),
        in_specs=[pl.BlockSpec(memory_space=pltpu.VMEM)] * 14,
        out_specs=(pl.BlockSpec(memory_space=pltpu.VMEM),) * 3,
        scratch_shapes=[pltpu.VMEM((rows, head), f32)] * 3 + [pltpu.VMEM((text_rows, head), f32)] * 2,
        compiler_params=pltpu.CompilerParams(vmem_limit_bytes=48 * 1024 * 1024),
        cost_estimate=pl.CostEstimate(
            flops=10 * rows * (rows + text_rows) * columns,
            bytes_accessed=12 * rows * columns * 4,
            transcendentals=heads * rows * (rows + text_rows),
        ),
        name="attention_backward",
    )(qkv, query, key, value, text, grad, lse, cross, cosine, sine, gains, mask, text_mask, gate)


def ffn_forward(ffn_in, weights):
    rows, width = ffn_in.shape
    units = weights.shape[1] // 2
    tile = min(units, 256)
    tiles = units // tile

    def kernel(in_ref, gate_ref, up_ref, hidden_ref, by_gate_ref, by_up_ref):
        gate_act = dot(in_ref[...], gate_ref[...])
        up_act = dot(in_ref[...], up_ref[...])
        sigmoid = 1.0 / (1.0 + jnp.exp(-gate_act))
        silu = gate_act * sigmoid
        hidden_ref[...] = (silu * up_act).astype(bf16)
        by_gate_ref[...] = up_act * sigmoid * (1.0 + gate_act * (1.0 - sigmoid))
        by_up_ref[...] = silu

    part = pl.BlockSpec((rows, tile), lambda j: (0, j))
    wide = jax.ShapeDtypeStruct((rows, units), f32)
    return pl.pallas_call(
        kernel,
        grid=(tiles,),
        out_shape=(jax.ShapeDtypeStruct((rows, units), bf16), wide, wide),
        in_specs=[
            pl.BlockSpec((rows, width), lambda j: (0, 0)),
            pl.BlockSpec((width, tile), lambda j: (0, j)),
            pl.BlockSpec((width, tile), lambda j: (0, tiles + j)),
        ],
        out_specs=(part, part, part),
        compiler_params=pltpu.CompilerParams(vmem_limit_bytes=48 * 1024 * 1024),
        cost_estimate=pl.CostEstimate(
            flops=4 * rows * width * units,
            bytes_accessed=2 * rows * width + 4 * width * units + 10 * rows * units,
            transcendentals=rows * units,
        ),
        name="ffn_forward",
    )(ffn_in, weights, weights)


def ffn_backward(back, down, weights, by_gate, by_up):
    rows, width = back.shape
    units = down.shape[1]
    tile = min(units, 256)
    tiles = units // tile

    def kernel(back_ref, down_ref, gate_ref, up_ref, by_gate_ref, by_up_ref, act_ref, grad_ref, total):
        step = pl.program_id(0)

        @pl.when(step == 0)
        def _():
            total[...] = jnp.zeros_like(total)

        grad_hidden = dot(back_ref[...], down_ref[...])
        grad_gate = (grad_hidden * by_gate_ref[...]).astype(bf16)
        grad_up = (grad_hidden * by_up_ref[...]).astype(bf16)
        act_ref[:, pl.ds(pl.multiple_of(step * tile, tile), tile)] = grad_gate
        act_ref[:, pl.ds(pl.multiple_of(units + step * tile, tile), tile)] = grad_up
        total[...] += dot_nt(grad_gate, gate_ref[...]) + dot_nt(grad_up, up_ref[...])

        @pl.when(step == tiles - 1)
        def _():
            grad_ref[...] = total[...].astype(bf16)

    whole = pl.BlockSpec((rows, width), lambda j: (0, 0))
    part = pl.BlockSpec((rows, tile), lambda j: (0, j))
    return pl.pallas_call(
        kernel,
        grid=(tiles,),
        out_shape=(
            jax.ShapeDtypeStruct((rows, 2 * units), bf16),
            jax.ShapeDtypeStruct((rows, width), bf16),
        ),
        in_specs=[
            whole,
            pl.BlockSpec((width, tile), lambda j: (0, j)),
            pl.BlockSpec((width, tile), lambda j: (0, j)),
            pl.BlockSpec((width, tile), lambda j: (0, tiles + j)),
            part,
            part,
        ],
        out_specs=(pl.BlockSpec((rows, 2 * units), lambda j: (0, 0)), whole),
        scratch_shapes=[pltpu.VMEM((rows, width), f32)],
        compiler_params=pltpu.CompilerParams(vmem_limit_bytes=48 * 1024 * 1024),
        cost_estimate=pl.CostEstimate(
            flops=6 * rows * width * units,
            bytes_accessed=6 * rows * width + 6 * width * units + 12 * rows * units,
            transcendentals=0,
        ),
        name="ffn_backward",
    )(back, down, weights, weights, by_gate, by_up)


def widen(block, parts):
    rows = block.shape[0]
    columns = block.shape[1] // parts

    def kernel(block_ref, *part_refs):
        for i, part_ref in enumerate(part_refs):
            part_ref[...] = block_ref[:, i * columns : (i + 1) * columns].astype(f32)

    return pl.pallas_call(
        kernel,
        out_shape=[jax.ShapeDtypeStruct((rows, columns), f32)] * parts,
        in_specs=[pl.BlockSpec(memory_space=pltpu.VMEM)],
        out_specs=[pl.BlockSpec(memory_space=pltpu.VMEM)] * parts,
        name="widen",
    )(block)


def build(n_f, n_s):
    n_z = n_f // 2
    swaps = [[(i, i ^ k) for i in range(n_s)] for k in range(n_s)]

    def twin(block):
        return lax.ppermute(block, "fsdp", [(i, i ^ 1) for i in range(n_f)])

    def fsdp_xor(block, k):
        return lax.ppermute(block, "fsdp", [(i, i ^ k) for i in range(n_f)])

    def after(block, *earlier):
        return lax.optimization_barrier((block,) + earlier)[0]

    def stage(*values):
        return lax.optimization_barrier(values)

    def fsdp_scatter(total):
        return lax.psum_scatter(total, "fsdp", scatter_dimension=0, tiled=True)

    class Gather:
        def __init__(self, own, core):
            got = twin(own)
            first = core == 0
            pair = [jnp.where(first, own, got), jnp.where(first, got, own)]
            self.got = [jnp.concatenate(pair, axis=0)]
            self.twins = [None]

        def step(self, last=None):
            last = n_z - 1 if last is None else last
            while len(self.got) <= last:
                k = len(self.got)
                pairs = [(2 * z, 2 * z + 2) for z in range(k - 1, n_z - 1)]
                pairs += [(2 * z + 1, 2 * z - 1) for z in range(1, n_z - k + 1)]
                self.got.append(lax.ppermute(self.got[-1], "fsdp", pairs))

        def pass_on(self, last=None):
            last = n_z - 1 if last is None else last
            while len(self.twins) <= last:
                self.twins.append(twin(self.got[len(self.twins)]))

        def full(self, chip, core):
            rows, columns = self.got[0].shape
            whole = jnp.zeros((n_z, rows, columns), self.got[0].dtype)
            for k in range(n_z):
                block = self.got[0] if k == 0 else self.got[k] + self.twins[n_z - k]
                at = jnp.where(core == 0, lax.rem(chip + n_z - k, n_z), lax.rem(chip + k, n_z))
                whole = lax.dynamic_update_slice(whole, block[None], (at, 0, 0))
            return whole.reshape(n_z * rows, columns)

    def seq_near(block):
        return [lax.ppermute(block, "seq", swaps[k]) for k in (1, 2)]

    def seq_far(near, axis=0):
        half = near[0].shape[axis] // 2
        return [
            lax.ppermute(lax.slice_in_dim(near[0], 0, half, axis=axis), "seq", swaps[2]),
            lax.ppermute(lax.slice_in_dim(near[1], half, 2 * half, axis=axis), "seq", swaps[1]),
        ]

    def seq_gather(block, axis=0):
        if n_s != 4:
            parts = [block] + [lax.ppermute(block, "seq", swaps[k]) for k in range(1, n_s)]
        else:
            near = seq_near(block)
            far = jnp.concatenate(seq_far(near, axis + 1 if axis else 0), axis=axis + 1) if axis else None
            parts = [block] + near + ([far] if axis else seq_far(near))
        return jnp.concatenate(parts, axis=axis)

    def seq_send(total, rows):
        return [
            lax.ppermute(total[k * rows : (k + 1) * rows].astype(bf16), "seq", swaps[k])
            for k in range(1, n_s)
        ]

    def seq_sum(total, parts, rows):
        result = total[:rows].astype(f32)
        for part in parts:
            result = result + part.astype(f32)
        return result

    def by_seq(stacked, index):
        bit = 1
        while bit < n_s:
            split = stacked.reshape((n_s // (2 * bit), 2, bit) + stacked.shape[1:])
            turn = (index & bit) != 0
            first = jnp.where(turn, split[:, 1], split[:, 0])
            second = jnp.where(turn, split[:, 0], split[:, 1])
            stacked = jnp.stack([first, second], axis=1).reshape(stacked.shape)
            bit *= 2
        return stacked

    def all_sum(block, axis, size):
        bit = 1
        while bit < size:
            block = block + lax.ppermute(block, axis, [(i, i ^ bit) for i in range(size)])
            bit *= 2
        return block

    def local(
        tokens,
        cotangent,
        condition,
        caption,
        positions,
        clip_lengths,
        caption_lengths,
        modulator,
        query_weight,
        key_weight,
        value_weight,
        output_weight,
        textkey_weight,
        textvalue_weight,
        gate_weight,
        up_weight,
        down_weight,
        attn_gain,
        ffn_gain,
        query_gain,
        key_gain,
        cross_gate,
    ):
        rows = tokens.shape[0]
        width = tokens.shape[1]
        head_size = query_gain.shape[0]
        columns = query_weight.shape[1]
        heads = columns // head_size
        units = gate_weight.shape[1]
        clip_rows = positions.shape[1]
        text_rows = caption.shape[0]
        seq_index = lax.axis_index("seq")
        fsdp_index = lax.axis_index("fsdp")
        length = clip_lengths[0]
        text_length = caption_lengths[0]
        scale = head_size ** (-0.5)

        chip = fsdp_index // 2
        core = fsdp_index % 2

        def fsdp_gather(*parts):
            return lax.all_gather(jnp.concatenate(parts, axis=1), "fsdp", axis=0, tiled=True)

        attn_full = fsdp_gather(query_weight, key_weight, value_weight, output_weight.T)
        qkv_full = attn_full[:, : 3 * columns]
        output_t = attn_full[:, 3 * columns :]
        cap_rows = text_rows // n_s
        cap_columns = textkey_weight.shape[0]
        cap_piece = lax.dynamic_slice_in_dim(caption, seq_index * cap_rows, cap_rows, 0)
        cap_mine = cap_piece.reshape(cap_rows, n_f, cap_columns).transpose(1, 0, 2)
        cap_mine = lax.all_to_all(cap_mine, "fsdp", 0, 0)
        cond_low = jax.nn.silu(after(condition, cap_mine).astype(f32)).astype(bf16)
        cond_all = cond_low
        bit = 1
        while bit < n_f:
            cond_all = jnp.concatenate([cond_all, fsdp_xor(cond_all, bit)], axis=0)
            bit *= 2
        tokens_all = seq_gather(tokens)
        mod_rows = modulator.shape[0]
        cond_mine = lax.dynamic_slice_in_dim(cond_all, fsdp_index * mod_rows, mod_rows, 1)
        mod_part = dot(cond_mine, modulator)
        half = n_f // 2
        while half:
            mod_part = mod_part[:half] + fsdp_xor(mod_part[half:], half)
            half //= 2
        cap_all = seq_gather(cap_mine[:, None], 1)
        modulation = mod_part
        bit = 1
        while bit < n_s:
            modulation = jnp.concatenate(
                [modulation, lax.ppermute(modulation, "seq", swaps[bit])], axis=0
            )
            bit *= 2
        modulation = by_seq(modulation, seq_index).reshape(-1)
        cap_all = cap_all.reshape(n_f * text_rows, cap_columns)
        text_own = jnp.concatenate([textkey_weight, textvalue_weight], axis=1)
        text_part = dot(cap_all, text_own).astype(bf16)
        text_both = fsdp_scatter(text_part)
        ffn_full = fsdp_gather(after(gate_weight, text_part), up_weight)
        down_t = lax.all_gather(down_weight.T, "fsdp", axis=0, tiled=True)
        tokens_all = tokens_all.astype(f32)
        cotangent_all = seq_gather(after(cotangent, cap_all)).astype(f32)

        scale_attn = modulation[:width]
        gate_attn = modulation[width : 2 * width]
        scale_ffn = modulation[2 * width : 3 * width]
        gate_ffn = modulation[3 * width :]
        tanh_attn = jnp.tanh(gate_attn)
        tanh_ffn = jnp.tanh(gate_ffn)

        order = [seq_index ^ k for k in range(n_s)]
        row_index = jnp.concatenate([order[k] * rows + jnp.arange(rows) for k in range(n_s)])
        text_index = jnp.concatenate(
            [order[k] * cap_rows + jnp.arange(cap_rows) for k in range(n_s)]
        )
        places = jnp.concatenate(
            [lax.dynamic_slice_in_dim(positions, order[k] * rows, rows, 1) for k in range(n_s)],
            axis=1,
        )

        inv_attn_all = lax.rsqrt(jnp.mean(tokens_all * tokens_all, axis=-1, keepdims=True) + epsilon)
        normed_all = (tokens_all * inv_attn_all * attn_gain * (1.0 + scale_attn)).astype(bf16)
        inputs = tokens.astype(f32)
        inv_attn = inv_attn_all[:rows]
        unit_attn = inputs * inv_attn
        qkv = dot(normed_all, qkv_full)
        cosine, sine = rope_tables(places, head_size)
        cosine = jnp.concatenate([cosine, cosine], axis=1)
        sine = jnp.concatenate([-sine, sine], axis=1)
        gains = jnp.zeros((8, head_size), f32).at[0].set(query_gain).at[1].set(key_gain)
        mask = jnp.where(row_index < length, 0.0, masked_score).astype(f32)[None, :]
        text_mask = jnp.where(text_index < text_length, 0.0, masked_score).astype(f32)[None, :]
        gate_heads = jnp.tanh(lax.dynamic_slice_in_dim(cross_gate, seq_index * heads, heads))
        gate_row = jnp.repeat(gate_heads, head_size)[None, :]
        query_rot, key_rot, value_low, mixed_rows, cross_out, lse = attention_forward(
            qkv, text_both, cosine, sine, gains, mask, text_mask, gate_row, heads, head_size
        )
        attn_sent = dot_nt(mixed_rows, output_t)
        attn_out = seq_sum(attn_sent, seq_send(attn_sent, rows), rows)
        branch_attn = tanh_attn * attn_out
        hidden_in = inputs + branch_attn
        inv_ffn = lax.rsqrt(jnp.mean(hidden_in * hidden_in, axis=-1, keepdims=True) + epsilon)
        unit_ffn = hidden_in * inv_ffn
        ffn_in = (unit_ffn * ffn_gain * (1.0 + scale_ffn)).astype(bf16)
        ffn_all = seq_gather(ffn_in)
        ffn_back_all = (tanh_ffn * cotangent_all).astype(bf16)
        hidden, by_gate, by_up = ffn_forward(ffn_all, ffn_full)
        down_part = dot_tn(ffn_back_all, hidden).astype(bf16)
        down_grads = fsdp_scatter(down_part)
        grad_act, grad_sent = ffn_backward(
            ffn_back_all, after(down_t, down_part), ffn_full, by_gate, by_up
        )
        parts = seq_send(grad_sent, rows)
        act_part = dot_tn(ffn_all, grad_act).astype(bf16)
        *parts, act_part = stage(*parts, act_part)
        act_grads = fsdp_scatter(after(act_part, down_grads))
        grad_ffn_in = seq_sum(grad_sent, parts, rows)
        grad_out = cotangent.astype(f32)
        grad_ffn_gain = jnp.sum(grad_ffn_in * unit_ffn * (1.0 + scale_ffn), axis=0)
        grad_scale_ffn = jnp.sum(grad_ffn_in * unit_ffn * ffn_gain, axis=0)
        scaled_ffn = grad_ffn_in * ffn_gain * (1.0 + scale_ffn)
        grad_hidden_in = grad_out + inv_ffn * (
            scaled_ffn - unit_ffn * jnp.mean(scaled_ffn * unit_ffn, axis=-1, keepdims=True)
        )
        attn_back = (tanh_attn * grad_hidden_in).astype(bf16)
        grad_gate_attn = jnp.sum(grad_hidden_in * attn_out, axis=0) * (1.0 - tanh_attn * tanh_attn)
        attn_back_all = seq_gather(attn_back)
        grad_mixed = dot(attn_back_all, output_t).astype(bf16)
        output_part = dot_tn(attn_back_all, mixed_rows).astype(bf16)
        ffn_sent = dot_nt(after(hidden, attn_back_all), down_t)
        ffn_parts = seq_send(ffn_sent, rows)
        qkv_rows, text_grads_rows, head_sums = attention_backward(
            qkv, query_rot, key_rot, value_low, text_both, grad_mixed, lse, cross_out,
            cosine, sine, gains, mask, text_mask, gate_row, heads, head_size,
        )
        qkv_rows, text_grads_rows, *ffn_parts = stage(qkv_rows, text_grads_rows, *ffn_parts)

        text_back = Gather(text_grads_rows, core)
        text_back.step(1)
        normed_sent = dot_nt(qkv_rows, qkv_full)
        parts = seq_send(normed_sent, rows)
        qkv_part = dot_tn(normed_all, after(qkv_rows, normed_sent)).astype(bf16)
        attn_part = jnp.concatenate([qkv_part, output_part], axis=1)
        ffn_out = seq_sum(ffn_sent, ffn_parts, rows)
        branch_ffn = tanh_ffn * ffn_out
        result = hidden_in + branch_ffn
        row_valid = (seq_index * rows + jnp.arange(rows) < length)[:, None]
        sums = jnp.stack(
            [
                jnp.sum(jnp.where(row_valid, result * result, 0.0)),
                jnp.sum(jnp.where(row_valid, branch_attn * branch_attn, 0.0)),
                jnp.sum(jnp.where(row_valid, branch_ffn * branch_ffn, 0.0)),
            ]
        )
        grad_gate_ffn = jnp.sum(grad_out * ffn_out, axis=0) * (1.0 - tanh_ffn * tanh_ffn)

        grad_query_gain = head_sums[0, :head_size]
        grad_key_gain = head_sums[1, :head_size]
        grad_gate_heads = jnp.sum(
            head_sums[2, :columns].reshape(heads, head_size), axis=1
        ) * (1.0 - gate_heads * gate_heads)
        attn_part, act_grads, text_back.got[1] = stage(attn_part, act_grads, text_back.got[1])
        attn_grads = fsdp_scatter(attn_part)
        act_grads = widen(act_grads, 2)
        down_grads = widen(down_grads, 1)[0]
        *parts, down_grads, gate_grads, up_grads = stage(*parts, down_grads, *act_grads)
        text_back.step()
        text_back.pass_on()
        grad_normed = seq_sum(normed_sent, parts, rows)
        grad_attn_gain = jnp.sum(grad_normed * unit_attn * (1.0 + scale_attn), axis=0)
        grad_scale_attn = jnp.sum(grad_normed * unit_attn * attn_gain, axis=0)
        scaled_attn = grad_normed * attn_gain * (1.0 + scale_attn)
        token_grad = grad_hidden_in + inv_attn * (
            scaled_attn - unit_attn * jnp.mean(scaled_attn * unit_attn, axis=-1, keepdims=True)
        )

        gate_heads_full = lax.dynamic_update_slice_in_dim(
            jnp.zeros_like(cross_gate), grad_gate_heads, seq_index * heads, 0
        )
        sizes = jnp.concatenate(
            [grad_attn_gain, grad_ffn_gain, gate_heads_full, grad_query_gain, grad_key_gain, sums]
        )
        sizes = all_sum(sizes, "seq", n_s)
        mod_grad = jnp.concatenate([grad_scale_attn, grad_gate_attn, grad_scale_ffn, grad_gate_ffn])
        mod_mine = by_seq(mod_grad.reshape(n_s, -1), seq_index)
        half = n_s // 2
        while half:
            mod_mine = mod_mine[:half] + lax.ppermute(mod_mine[half:], "seq", swaps[half])
            half //= 2
        mod_mine = mod_mine.astype(bf16)
        bit = 1
        while bit < n_f:
            mod_mine = jnp.concatenate([mod_mine, fsdp_xor(mod_mine, bit)], axis=0)
            bit *= 2
        modulator_grad = dot_tn(cond_mine, mod_mine)
        totals = sizes[-3:]
        residual_rms = jnp.sqrt(totals / (length.astype(f32) * width))[:, None]
        small = all_sum(sizes[:-3], "fsdp", n_f)
        text_grads = dot_tn(cap_all, text_back.full(chip, core))
        attn_grads = widen(attn_grads, 4)
        n_heads = cross_gate.shape[0]
        ends = [width, width, n_heads, head_size, head_size]
        ends = [sum(ends[:i]) for i in range(6)]
        small = [small[ends[i] : ends[i + 1]] for i in range(5)]
        small = (small[0], small[1], small[3], small[4], small[2])
        return (
            result.astype(bf16),
            token_grad,
            modulator_grad,
            *attn_grads[:3],
            attn_grads[3].T,
            text_grads[:, :columns],
            text_grads[:, columns:],
            gate_grads,
            up_grads,
            down_grads.T,
            small[0],
            small[1],
            small[2],
            small[3],
            small[4],
            residual_rms,
        )

    return local


def solution(mesh):
    by_both = P(("fsdp", "seq"), None)
    return jax.shard_map(
        build(mesh.shape["fsdp"], mesh.shape["seq"]),
        mesh=mesh,
        in_specs=(
            by_both,
            by_both,
            P("fsdp", None),
            P("fsdp", None),
            P(None, "fsdp"),
            P("fsdp"),
            P("fsdp"),
            P("fsdp", "seq"),
            P("fsdp", "seq"),
            P("fsdp", "seq"),
            P("fsdp", "seq"),
            P("seq", "fsdp"),
            P("fsdp", "seq"),
            P("fsdp", "seq"),
            P("fsdp", "seq"),
            P("fsdp", "seq"),
            P("seq", "fsdp"),
            P(),
            P(),
            P(),
            P(),
            P(),
        ),
        out_specs=(
            by_both,
            by_both,
            P("fsdp", "seq"),
            P("fsdp", "seq"),
            P("fsdp", "seq"),
            P("fsdp", "seq"),
            P("seq", "fsdp"),
            P("fsdp", "seq"),
            P("fsdp", "seq"),
            P("fsdp", "seq"),
            P("fsdp", "seq"),
            P("seq", "fsdp"),
            P(),
            P(),
            P(),
            P(),
            P(),
            P(None, "fsdp"),
        ),
        check_vma=False,
    )
```

```python
import math

import jax
import jax.numpy as jnp
from jax import lax
from jax.experimental import pallas as pl
from jax.experimental.pallas import tpu as pltpu
from jax.sharding import PartitionSpec as P

epsilon = 1e-06
masked_score = -1e30
f32 = jnp.float32
bf16 = jnp.bfloat16


def rope_tables(positions, head_size):
    half = head_size // 2
    pair_index = jnp.arange(half)
    frequency = jnp.exp(pair_index.astype(f32) * (-2.0 * math.log(10000.0) / head_size))
    angle = jnp.zeros((positions.shape[1], half), f32)
    for axis_number in range(3):
        chosen = jnp.where(pair_index % 3 == axis_number, frequency, jnp.zeros_like(frequency))
        angle = angle + positions[axis_number].astype(f32)[:, None] * chosen[None, :]
    return (jnp.cos(angle), jnp.sin(angle))


def dot(left, right):
    return jnp.dot(left, right, preferred_element_type=f32)


def dot_nt(left, right):
    return lax.dot_general(left, right, (((1,), (1,)), ((), ())), preferred_element_type=f32)


def dot_tn(left, right):
    return lax.dot_general(left, right, (((0,), (0,)), ((), ())), preferred_element_type=f32)


def attention_forward(qkv, text, cosine, sine, gains, mask, text_mask, gate, heads, head):
    rows = qkv.shape[0]
    columns = heads * head
    block = min(rows, 256)

    def kernel(qkv_ref, text_ref, cos_ref, sin_ref, gain_ref, mask_ref, tmask_ref, gate_ref,
               q_ref, k_ref, v_ref, mixed_ref, cross_ref, lse_ref):
        cos = cos_ref[...]
        sin = sin_ref[...]
        lse_ref[...] = jnp.zeros_like(lse_ref)

        def turned(raw, gain):
            inverse = lax.rsqrt(jnp.mean(raw * raw, axis=-1, keepdims=True) + epsilon)
            value = raw * inverse * gain
            swapped = jnp.concatenate([value[:, head // 2 :], value[:, : head // 2]], axis=1)
            return (value * cos + swapped * sin).astype(bf16)

        for h in range(heads):
            at = slice(h * head, (h + 1) * head)
            q_ref[:, at] = turned(qkv_ref[:, at], gain_ref[0:1, :head])
            k_ref[:, at] = turned(
                qkv_ref[:, columns + h * head : columns + (h + 1) * head], gain_ref[1:2, :head]
            )
            v_ref[:, at] = qkv_ref[:, 2 * columns + h * head : 2 * columns + (h + 1) * head].astype(bf16)

        def attend(query, keys, values, masks):
            scores = dot_nt(query, keys) + masks
            peak = jnp.max(scores, axis=-1, keepdims=True)
            expo = jnp.exp(scores - peak)
            total = jnp.sum(expo, axis=-1, keepdims=True)
            return dot(expo.astype(bf16), values) / total, peak + jnp.log(total)

        for h in range(heads):
            at = slice(h * head, (h + 1) * head)
            keys = k_ref[:, at]
            values = v_ref[:, at]
            text_keys = text_ref[:, at]
            text_values = text_ref[:, columns + h * head : columns + (h + 1) * head]
            for b in range(rows // block):
                here = slice(b * block, (b + 1) * block)
                query = q_ref[here, at] * jnp.asarray(head**-0.5, bf16)
                own, own_lse = attend(query, keys, values, mask_ref[...])
                other, other_lse = attend(query, text_keys, text_values, tmask_ref[...])
                cross_ref[here, at] = other
                mixed_ref[here, at] = (own + gate_ref[:, at] * other).astype(bf16)
                lse_ref[here, h : h + 1] = own_lse
                lse_ref[here, heads + h : heads + h + 1] = other_lse

    wide = jax.ShapeDtypeStruct((rows, columns), bf16)
    return pl.pallas_call(
        kernel,
        out_shape=(wide, wide, wide, wide, jax.ShapeDtypeStruct((rows, columns), f32),
                   jax.ShapeDtypeStruct((rows, 128), f32)),
        in_specs=[pl.BlockSpec(memory_space=pltpu.VMEM)] * 8,
        out_specs=(pl.BlockSpec(memory_space=pltpu.VMEM),) * 6,
        compiler_params=pltpu.CompilerParams(vmem_limit_bytes=48 * 1024 * 1024),
        cost_estimate=pl.CostEstimate(
            flops=4 * rows * (rows + text.shape[0]) * columns,
            bytes_accessed=8 * rows * columns * 4,
            transcendentals=heads * rows * (rows + text.shape[0]),
        ),
        name="attention_forward",
    )(qkv, text, cosine, sine, gains, mask, text_mask, gate)


def soft_back(query, keys, values, masks, lse, back):
    probs = jnp.exp(dot_nt(query, keys) + masks - lse)
    grad_probs = dot_nt(back, values)
    delta = jnp.sum(probs * grad_probs, axis=-1, keepdims=True)
    return probs.astype(bf16), (probs * (grad_probs - delta)).astype(bf16)


def cross_backward(query, text, grad, lse, cross, text_mask, gate, heads, head):
    rows = query.shape[0]
    text_rows = text.shape[0]
    columns = heads * head
    block = min(rows, 256)
    scale = head**-0.5

    def kernel(q_ref, text_ref, grad_ref, lse_ref, cross_ref, tmask_ref, gate_ref,
               text_rows_ref, dq_ref, small_ref, dtk_ref, dtv_ref):
        small_ref[...] = jnp.zeros_like(small_ref)
        for h in range(heads):
            at = slice(h * head, (h + 1) * head)
            at_value = slice(columns + h * head, columns + (h + 1) * head)
            text_keys = text_ref[:, at]
            text_values = text_ref[:, at_value]
            for b in range(rows // block):
                here = slice(b * block, (b + 1) * block)
                query = q_ref[here, at] * jnp.asarray(scale, bf16)
                wide = grad_ref[here, at].astype(f32)
                cross_back = (wide * gate_ref[:, at]).astype(bf16)
                probs, grads = soft_back(
                    query, text_keys, text_values, tmask_ref[...],
                    lse_ref[here, heads + h : heads + h + 1], cross_back,
                )
                dq_ref[here, at] = dot(grads, text_keys)
                dtk = dot_tn(grads, query)
                dtv = dot_tn(probs, cross_back)
                small_ref[0:1, at] += jnp.sum(wide * cross_ref[here, at], axis=0, keepdims=True)
                if b == 0:
                    dtk_ref[...] = dtk
                    dtv_ref[...] = dtv
                else:
                    dtk_ref[...] += dtk
                    dtv_ref[...] += dtv
            text_rows_ref[:, at] = dtk_ref[...].astype(bf16)
            text_rows_ref[:, at_value] = dtv_ref[...].astype(bf16)

    return pl.pallas_call(
        kernel,
        out_shape=(
            jax.ShapeDtypeStruct((text_rows, 2 * columns), bf16),
            jax.ShapeDtypeStruct((rows, columns), f32),
            jax.ShapeDtypeStruct((8, columns), f32),
        ),
        in_specs=[pl.BlockSpec(memory_space=pltpu.VMEM)] * 7,
        out_specs=(pl.BlockSpec(memory_space=pltpu.VMEM),) * 3,
        scratch_shapes=[pltpu.VMEM((text_rows, head), f32)] * 2,
        compiler_params=pltpu.CompilerParams(vmem_limit_bytes=48 * 1024 * 1024),
        cost_estimate=pl.CostEstimate(
            flops=10 * rows * text_rows * columns,
            bytes_accessed=6 * rows * columns * 4,
            transcendentals=heads * rows * text_rows,
        ),
        name="cross_backward",
    )(query, text, grad, lse, cross, text_mask, gate)


def self_backward(qkv, query, key, value, grad, lse, cross_query, cosine, sine, gains, mask, heads, head):
    rows = qkv.shape[0]
    columns = heads * head
    block = min(rows, 256)
    scale = head**-0.5

    def kernel(qkv_ref, q_ref, k_ref, v_ref, grad_ref, lse_ref, cross_ref, cos_ref, sin_ref,
               gain_ref, mask_ref, rows_ref, small_ref, dq_ref, dk_ref, dv_ref):
        cos = cos_ref[...]
        sin = sin_ref[...]
        small_ref[...] = jnp.zeros_like(small_ref)

        def raw_back(grad, raw, gain, row):
            swapped = jnp.concatenate([grad[:, head // 2 :], grad[:, : head // 2]], axis=1)
            turned = grad * cos - swapped * sin
            inverse = lax.rsqrt(jnp.mean(raw * raw, axis=-1, keepdims=True) + epsilon)
            unit = raw * inverse
            small_ref[row : row + 1, :head] += jnp.sum(turned * unit, axis=0, keepdims=True)
            scaled = turned * gain
            return (
                inverse * (scaled - unit * jnp.mean(scaled * unit, axis=-1, keepdims=True))
            ).astype(bf16)

        for h in range(heads):
            at = slice(h * head, (h + 1) * head)
            at_key = slice(columns + h * head, columns + (h + 1) * head)
            at_value = slice(2 * columns + h * head, 2 * columns + (h + 1) * head)
            keys = k_ref[:, at]
            values = v_ref[:, at]
            for b in range(rows // block):
                here = slice(b * block, (b + 1) * block)
                query = q_ref[here, at] * jnp.asarray(scale, bf16)
                back = grad_ref[here, at]
                probs, grads = soft_back(
                    query, keys, values, mask_ref[...], lse_ref[here, h : h + 1], back
                )
                dq_ref[here, :] = (dot(grads, keys) + cross_ref[here, at]) * scale
                dk = dot_tn(grads, query)
                dv = dot_tn(probs, back)
                if b == 0:
                    dk_ref[...] = dk
                    dv_ref[...] = dv
                else:
                    dk_ref[...] += dk
                    dv_ref[...] += dv
            rows_ref[:, at] = raw_back(dq_ref[...], qkv_ref[:, at], gain_ref[0:1, :head], 0)
            rows_ref[:, at_key] = raw_back(dk_ref[...], qkv_ref[:, at_key], gain_ref[1:2, :head], 1)
            rows_ref[:, at_value] = dv_ref[...].astype(bf16)

    return pl.pallas_call(
        kernel,
        out_shape=(
            jax.ShapeDtypeStruct((rows, 3 * columns), bf16),
            jax.ShapeDtypeStruct((8, 128), f32),
        ),
        in_specs=[pl.BlockSpec(memory_space=pltpu.VMEM)] * 11,
        out_specs=(pl.BlockSpec(memory_space=pltpu.VMEM),) * 2,
        scratch_shapes=[pltpu.VMEM((rows, head), f32)] * 3,
        compiler_params=pltpu.CompilerParams(vmem_limit_bytes=48 * 1024 * 1024),
        cost_estimate=pl.CostEstimate(
            flops=10 * rows * rows * columns,
            bytes_accessed=10 * rows * columns * 4,
            transcendentals=heads * rows * rows,
        ),
        name="self_backward",
    )(qkv, query, key, value, grad, lse, cross_query, cosine, sine, gains, mask)


def ffn_forward(ffn_in, weights):
    rows, width = ffn_in.shape
    units = weights.shape[1] // 2
    tile = min(units, 256)
    tiles = units // tile

    def kernel(in_ref, gate_ref, up_ref, hidden_ref, by_gate_ref, by_up_ref):
        gate_act = dot(in_ref[...], gate_ref[...])
        up_act = dot(in_ref[...], up_ref[...])
        sigmoid = 1.0 / (1.0 + jnp.exp(-gate_act))
        silu = gate_act * sigmoid
        hidden_ref[...] = (silu * up_act).astype(bf16)
        by_gate_ref[...] = up_act * sigmoid * (1.0 + gate_act * (1.0 - sigmoid))
        by_up_ref[...] = silu

    part = pl.BlockSpec((rows, tile), lambda j: (0, j))
    wide = jax.ShapeDtypeStruct((rows, units), f32)
    return pl.pallas_call(
        kernel,
        grid=(tiles,),
        out_shape=(jax.ShapeDtypeStruct((rows, units), bf16), wide, wide),
        in_specs=[
            pl.BlockSpec((rows, width), lambda j: (0, 0)),
            pl.BlockSpec((width, tile), lambda j: (0, j)),
            pl.BlockSpec((width, tile), lambda j: (0, tiles + j)),
        ],
        out_specs=(part, part, part),
        compiler_params=pltpu.CompilerParams(vmem_limit_bytes=48 * 1024 * 1024),
        cost_estimate=pl.CostEstimate(
            flops=4 * rows * width * units,
            bytes_accessed=2 * rows * width + 4 * width * units + 10 * rows * units,
            transcendentals=rows * units,
        ),
        name="ffn_forward",
    )(ffn_in, weights, weights)


def ffn_backward(back, down, weights, by_gate, by_up):
    rows, width = back.shape
    units = down.shape[1]
    tile = min(units, 256)
    tiles = units // tile

    def kernel(back_ref, down_ref, gate_ref, up_ref, by_gate_ref, by_up_ref, act_ref, grad_ref, total):
        step = pl.program_id(0)

        @pl.when(step == 0)
        def _():
            total[...] = jnp.zeros_like(total)

        grad_hidden = dot(back_ref[...], down_ref[...])
        grad_gate = (grad_hidden * by_gate_ref[...]).astype(bf16)
        grad_up = (grad_hidden * by_up_ref[...]).astype(bf16)
        act_ref[:, pl.ds(pl.multiple_of(step * tile, tile), tile)] = grad_gate
        act_ref[:, pl.ds(pl.multiple_of(units + step * tile, tile), tile)] = grad_up
        total[...] += dot_nt(grad_gate, gate_ref[...]) + dot_nt(grad_up, up_ref[...])

        @pl.when(step == tiles - 1)
        def _():
            grad_ref[...] = total[...].astype(bf16)

    whole = pl.BlockSpec((rows, width), lambda j: (0, 0))
    part = pl.BlockSpec((rows, tile), lambda j: (0, j))
    return pl.pallas_call(
        kernel,
        grid=(tiles,),
        out_shape=(
            jax.ShapeDtypeStruct((rows, 2 * units), bf16),
            jax.ShapeDtypeStruct((rows, width), bf16),
        ),
        in_specs=[
            whole,
            pl.BlockSpec((width, tile), lambda j: (0, j)),
            pl.BlockSpec((width, tile), lambda j: (0, j)),
            pl.BlockSpec((width, tile), lambda j: (0, tiles + j)),
            part,
            part,
        ],
        out_specs=(pl.BlockSpec((rows, 2 * units), lambda j: (0, 0)), whole),
        scratch_shapes=[pltpu.VMEM((rows, width), f32)],
        compiler_params=pltpu.CompilerParams(vmem_limit_bytes=48 * 1024 * 1024),
        cost_estimate=pl.CostEstimate(
            flops=6 * rows * width * units,
            bytes_accessed=6 * rows * width + 6 * width * units + 12 * rows * units,
            transcendentals=0,
        ),
        name="ffn_backward",
    )(back, down, weights, weights, by_gate, by_up)


def widen(block, parts):
    rows = block.shape[0]
    columns = block.shape[1] // parts

    def kernel(block_ref, *part_refs):
        for i, part_ref in enumerate(part_refs):
            part_ref[...] = block_ref[:, i * columns : (i + 1) * columns].astype(f32)

    return pl.pallas_call(
        kernel,
        out_shape=[jax.ShapeDtypeStruct((rows, columns), f32)] * parts,
        in_specs=[pl.BlockSpec(memory_space=pltpu.VMEM)],
        out_specs=[pl.BlockSpec(memory_space=pltpu.VMEM)] * parts,
        name="widen",
    )(block)


def build(n_f, n_s):
    n_z = n_f // 2
    swaps = [[(i, i ^ k) for i in range(n_s)] for k in range(n_s)]

    def twin(block):
        return lax.ppermute(block, "fsdp", [(i, i ^ 1) for i in range(n_f)])

    def fsdp_xor(block, k):
        return lax.ppermute(block, "fsdp", [(i, i ^ k) for i in range(n_f)])

    def after(block, *earlier):
        return lax.optimization_barrier((block,) + earlier)[0]

    def stage(*values):
        return lax.optimization_barrier(values)

    def fsdp_scatter(total):
        return lax.psum_scatter(total, "fsdp", scatter_dimension=0, tiled=True)

    class Gather:
        def __init__(self, own, core):
            got = twin(own)
            first = core == 0
            pair = [jnp.where(first, own, got), jnp.where(first, got, own)]
            self.got = [jnp.concatenate(pair, axis=0)]
            self.twins = [None]

        def step(self, last=None):
            last = n_z - 1 if last is None else last
            while len(self.got) <= last:
                k = len(self.got)
                pairs = [(2 * z, 2 * z + 2) for z in range(k - 1, n_z - 1)]
                pairs += [(2 * z + 1, 2 * z - 1) for z in range(1, n_z - k + 1)]
                self.got.append(lax.ppermute(self.got[-1], "fsdp", pairs))

        def pass_on(self, last=None):
            last = n_z - 1 if last is None else last
            while len(self.twins) <= last:
                self.twins.append(twin(self.got[len(self.twins)]))

        def full(self, chip, core):
            rows, columns = self.got[0].shape
            whole = jnp.zeros((n_z, rows, columns), self.got[0].dtype)
            for k in range(n_z):
                block = self.got[0] if k == 0 else self.got[k] + self.twins[n_z - k]
                at = jnp.where(core == 0, lax.rem(chip + n_z - k, n_z), lax.rem(chip + k, n_z))
                whole = lax.dynamic_update_slice(whole, block[None], (at, 0, 0))
            return whole.reshape(n_z * rows, columns)

    def seq_near(block):
        return [lax.ppermute(block, "seq", swaps[k]) for k in (1, 2)]

    def seq_far(near, axis=0):
        half = near[0].shape[axis] // 2
        return [
            lax.ppermute(lax.slice_in_dim(near[0], 0, half, axis=axis), "seq", swaps[2]),
            lax.ppermute(lax.slice_in_dim(near[1], half, 2 * half, axis=axis), "seq", swaps[1]),
        ]

    def seq_gather(block, axis=0):
        if n_s != 4:
            parts = [block] + [lax.ppermute(block, "seq", swaps[k]) for k in range(1, n_s)]
        else:
            near = seq_near(block)
            far = jnp.concatenate(seq_far(near, axis + 1 if axis else 0), axis=axis + 1) if axis else None
            parts = [block] + near + ([far] if axis else seq_far(near))
        return jnp.concatenate(parts, axis=axis)

    def seq_send(total, rows):
        return [
            lax.ppermute(total[k * rows : (k + 1) * rows].astype(bf16), "seq", swaps[k])
            for k in range(1, n_s)
        ]

    def seq_sum(total, parts, rows):
        result = total[:rows].astype(f32)
        for part in parts:
            result = result + part.astype(f32)
        return result

    def by_seq(stacked, index):
        bit = 1
        while bit < n_s:
            split = stacked.reshape((n_s // (2 * bit), 2, bit) + stacked.shape[1:])
            turn = (index & bit) != 0
            first = jnp.where(turn, split[:, 1], split[:, 0])
            second = jnp.where(turn, split[:, 0], split[:, 1])
            stacked = jnp.stack([first, second], axis=1).reshape(stacked.shape)
            bit *= 2
        return stacked

    def all_sum(block, axis, size):
        bit = 1
        while bit < size:
            block = block + lax.ppermute(block, axis, [(i, i ^ bit) for i in range(size)])
            bit *= 2
        return block

    def local(
        tokens,
        cotangent,
        condition,
        caption,
        positions,
        clip_lengths,
        caption_lengths,
        modulator,
        query_weight,
        key_weight,
        value_weight,
        output_weight,
        textkey_weight,
        textvalue_weight,
        gate_weight,
        up_weight,
        down_weight,
        attn_gain,
        ffn_gain,
        query_gain,
        key_gain,
        cross_gate,
    ):
        rows = tokens.shape[0]
        width = tokens.shape[1]
        head_size = query_gain.shape[0]
        columns = query_weight.shape[1]
        heads = columns // head_size
        units = gate_weight.shape[1]
        clip_rows = positions.shape[1]
        text_rows = caption.shape[0]
        seq_index = lax.axis_index("seq")
        fsdp_index = lax.axis_index("fsdp")
        length = clip_lengths[0]
        text_length = caption_lengths[0]
        scale = head_size ** (-0.5)

        chip = fsdp_index // 2
        core = fsdp_index % 2

        def fsdp_gather(*parts):
            return lax.all_gather(jnp.concatenate(parts, axis=1), "fsdp", axis=0, tiled=True)

        attn_full = fsdp_gather(query_weight, key_weight, value_weight, output_weight.T)
        qkv_full = attn_full[:, : 3 * columns]
        output_t = attn_full[:, 3 * columns :]
        cap_rows = text_rows // n_s
        cap_columns = textkey_weight.shape[0]
        cap_piece = lax.dynamic_slice_in_dim(caption, seq_index * cap_rows, cap_rows, 0)
        cap_mine = cap_piece.reshape(cap_rows, n_f, cap_columns).transpose(1, 0, 2)
        cap_mine = lax.all_to_all(cap_mine, "fsdp", 0, 0)
        cond_low = jax.nn.silu(after(condition, cap_mine).astype(f32)).astype(bf16)
        cond_all = cond_low
        bit = 1
        while bit < n_f:
            cond_all = jnp.concatenate([cond_all, fsdp_xor(cond_all, bit)], axis=0)
            bit *= 2
        tokens_all = seq_gather(tokens)
        mod_rows = modulator.shape[0]
        cond_mine = lax.dynamic_slice_in_dim(cond_all, fsdp_index * mod_rows, mod_rows, 1)
        mod_part = dot(cond_mine, modulator)
        half = n_f // 2
        while half:
            mod_part = mod_part[:half] + fsdp_xor(mod_part[half:], half)
            half //= 2
        cap_all = seq_gather(cap_mine[:, None], 1)
        modulation = mod_part
        bit = 1
        while bit < n_s:
            modulation = jnp.concatenate(
                [modulation, lax.ppermute(modulation, "seq", swaps[bit])], axis=0
            )
            bit *= 2
        modulation = by_seq(modulation, seq_index).reshape(-1)
        cap_all = cap_all.reshape(n_f * text_rows, cap_columns)
        text_own = jnp.concatenate([textkey_weight, textvalue_weight], axis=1)
        text_part = dot(cap_all, text_own).astype(bf16)
        text_both = fsdp_scatter(text_part)
        ffn_full = fsdp_gather(after(gate_weight, text_part), up_weight)
        down_t = lax.all_gather(down_weight.T, "fsdp", axis=0, tiled=True)
        tokens_all = tokens_all.astype(f32)
        cotangent_all = seq_gather(after(cotangent, cap_all)).astype(f32)

        scale_attn = modulation[:width]
        gate_attn = modulation[width : 2 * width]
        scale_ffn = modulation[2 * width : 3 * width]
        gate_ffn = modulation[3 * width :]
        tanh_attn = jnp.tanh(gate_attn)
        tanh_ffn = jnp.tanh(gate_ffn)

        order = [seq_index ^ k for k in range(n_s)]
        row_index = jnp.concatenate([order[k] * rows + jnp.arange(rows) for k in range(n_s)])
        text_index = jnp.concatenate(
            [order[k] * cap_rows + jnp.arange(cap_rows) for k in range(n_s)]
        )
        places = jnp.concatenate(
            [lax.dynamic_slice_in_dim(positions, order[k] * rows, rows, 1) for k in range(n_s)],
            axis=1,
        )

        inv_attn_all = lax.rsqrt(jnp.mean(tokens_all * tokens_all, axis=-1, keepdims=True) + epsilon)
        normed_all = (tokens_all * inv_attn_all * attn_gain * (1.0 + scale_attn)).astype(bf16)
        inputs = tokens.astype(f32)
        inv_attn = inv_attn_all[:rows]
        unit_attn = inputs * inv_attn
        qkv = dot(normed_all, qkv_full)
        cosine, sine = rope_tables(places, head_size)
        cosine = jnp.concatenate([cosine, cosine], axis=1)
        sine = jnp.concatenate([-sine, sine], axis=1)
        gains = jnp.zeros((8, head_size), f32).at[0].set(query_gain).at[1].set(key_gain)
        mask = jnp.where(row_index < length, 0.0, masked_score).astype(f32)[None, :]
        text_mask = jnp.where(text_index < text_length, 0.0, masked_score).astype(f32)[None, :]
        gate_heads = jnp.tanh(lax.dynamic_slice_in_dim(cross_gate, seq_index * heads, heads))
        gate_row = jnp.repeat(gate_heads, head_size)[None, :]
        query_rot, key_rot, value_low, mixed_rows, cross_out, lse = attention_forward(
            qkv, text_both, cosine, sine, gains, mask, text_mask, gate_row, heads, head_size
        )
        attn_sent = dot_nt(mixed_rows, output_t)
        attn_out = seq_sum(attn_sent, seq_send(attn_sent, rows), rows)
        branch_attn = tanh_attn * attn_out
        hidden_in = inputs + branch_attn
        inv_ffn = lax.rsqrt(jnp.mean(hidden_in * hidden_in, axis=-1, keepdims=True) + epsilon)
        unit_ffn = hidden_in * inv_ffn
        ffn_in = (unit_ffn * ffn_gain * (1.0 + scale_ffn)).astype(bf16)
        ffn_all = seq_gather(ffn_in)
        ffn_back_all = (tanh_ffn * cotangent_all).astype(bf16)
        hidden, by_gate, by_up = ffn_forward(ffn_all, ffn_full)
        down_part = dot_tn(ffn_back_all, hidden).astype(bf16)
        down_grads = fsdp_scatter(down_part)
        grad_act, grad_sent = ffn_backward(
            ffn_back_all, after(down_t, down_part), ffn_full, by_gate, by_up
        )
        parts = seq_send(grad_sent, rows)
        act_part = dot_tn(ffn_all, grad_act).astype(bf16)
        *parts, act_part = stage(*parts, act_part)
        grad_ffn_in = seq_sum(grad_sent, parts, rows)
        grad_out = cotangent.astype(f32)
        grad_ffn_gain = jnp.sum(grad_ffn_in * unit_ffn * (1.0 + scale_ffn), axis=0)
        grad_scale_ffn = jnp.sum(grad_ffn_in * unit_ffn * ffn_gain, axis=0)
        scaled_ffn = grad_ffn_in * ffn_gain * (1.0 + scale_ffn)
        grad_hidden_in = grad_out + inv_ffn * (
            scaled_ffn - unit_ffn * jnp.mean(scaled_ffn * unit_ffn, axis=-1, keepdims=True)
        )
        attn_back = (tanh_attn * grad_hidden_in).astype(bf16)
        grad_gate_attn = jnp.sum(grad_hidden_in * attn_out, axis=0) * (1.0 - tanh_attn * tanh_attn)
        attn_back, act_part = stage(attn_back, act_part)
        act_grads = fsdp_scatter(after(act_part, down_grads))
        attn_back_all = seq_gather(attn_back)
        grad_mixed = dot(attn_back_all, output_t).astype(bf16)
        output_part = dot_tn(attn_back_all, mixed_rows).astype(bf16)
        ffn_sent = dot_nt(after(hidden, attn_back_all), down_t)
        ffn_parts = seq_send(ffn_sent, rows)
        text_grads_rows, cross_query, gate_sums = cross_backward(
            query_rot, text_both, grad_mixed, lse, cross_out, text_mask, gate_row, heads, head_size
        )
        text_back = Gather(text_grads_rows, core)
        cross_query, text_back.got[0] = stage(cross_query, text_back.got[0])
        text_back.step(1)
        qkv_rows, head_sums = self_backward(
            qkv, query_rot, key_rot, value_low, grad_mixed, lse, cross_query,
            cosine, sine, gains, mask, heads, head_size,
        )
        qkv_rows, text_back.got[1], *ffn_parts = stage(qkv_rows, text_back.got[1], *ffn_parts)
        text_back.step(2)
        text_back.pass_on(1)
        normed_sent = dot_nt(qkv_rows, qkv_full)
        parts = seq_send(normed_sent, rows)
        qkv_part = dot_tn(normed_all, after(qkv_rows, normed_sent)).astype(bf16)
        qkv_part, text_back.got[2], text_back.twins[1] = stage(
            qkv_part, text_back.got[2], text_back.twins[1]
        )
        text_back.step()
        text_back.pass_on(2)
        attn_part = jnp.concatenate([qkv_part, output_part], axis=1)
        ffn_out = seq_sum(ffn_sent, ffn_parts, rows)
        branch_ffn = tanh_ffn * ffn_out
        result = hidden_in + branch_ffn
        row_valid = (seq_index * rows + jnp.arange(rows) < length)[:, None]
        sums = jnp.stack(
            [
                jnp.sum(jnp.where(row_valid, result * result, 0.0)),
                jnp.sum(jnp.where(row_valid, branch_attn * branch_attn, 0.0)),
                jnp.sum(jnp.where(row_valid, branch_ffn * branch_ffn, 0.0)),
            ]
        )
        grad_gate_ffn = jnp.sum(grad_out * ffn_out, axis=0) * (1.0 - tanh_ffn * tanh_ffn)

        grad_query_gain = head_sums[0, :head_size]
        grad_key_gain = head_sums[1, :head_size]
        grad_gate_heads = jnp.sum(
            gate_sums[0].reshape(heads, head_size), axis=1
        ) * (1.0 - gate_heads * gate_heads)
        attn_part, act_grads, text_back.got[-1], parts[0] = stage(
            attn_part, act_grads, text_back.got[-1], parts[0]
        )
        text_back.pass_on()
        text_grads = dot_tn(cap_all, text_back.full(chip, core))
        attn_grads = fsdp_scatter(attn_part)
        act_grads = widen(act_grads, 2)
        down_grads = widen(down_grads, 1)[0]
        *parts, text_grads, down_grads, gate_grads, up_grads = stage(
            *parts, text_grads, down_grads, *act_grads
        )
        grad_normed = seq_sum(normed_sent, parts, rows)
        grad_attn_gain = jnp.sum(grad_normed * unit_attn * (1.0 + scale_attn), axis=0)
        grad_scale_attn = jnp.sum(grad_normed * unit_attn * attn_gain, axis=0)
        scaled_attn = grad_normed * attn_gain * (1.0 + scale_attn)
        token_grad = grad_hidden_in + inv_attn * (
            scaled_attn - unit_attn * jnp.mean(scaled_attn * unit_attn, axis=-1, keepdims=True)
        )

        gate_heads_full = lax.dynamic_update_slice_in_dim(
            jnp.zeros_like(cross_gate), grad_gate_heads, seq_index * heads, 0
        )
        sizes = jnp.concatenate(
            [grad_attn_gain, grad_ffn_gain, gate_heads_full, grad_query_gain, grad_key_gain, sums]
        )
        sizes = all_sum(sizes, "seq", n_s)
        mod_grad = jnp.concatenate([grad_scale_attn, grad_gate_attn, grad_scale_ffn, grad_gate_ffn])
        mod_mine = by_seq(mod_grad.reshape(n_s, -1), seq_index)
        half = n_s // 2
        while half:
            mod_mine = mod_mine[:half] + lax.ppermute(mod_mine[half:], "seq", swaps[half])
            half //= 2
        mod_mine = mod_mine.astype(bf16)
        bit = 1
        while bit < n_f:
            mod_mine = jnp.concatenate([mod_mine, fsdp_xor(mod_mine, bit)], axis=0)
            bit *= 2
        modulator_grad = dot_tn(cond_mine, mod_mine)
        totals = sizes[-3:]
        residual_rms = jnp.sqrt(totals / (length.astype(f32) * width))[:, None]
        small = all_sum(sizes[:-3], "fsdp", n_f)
        attn_grads = widen(attn_grads, 4)
        n_heads = cross_gate.shape[0]
        ends = [width, width, n_heads, head_size, head_size]
        ends = [sum(ends[:i]) for i in range(6)]
        small = [small[ends[i] : ends[i + 1]] for i in range(5)]
        small = (small[0], small[1], small[3], small[4], small[2])
        return (
            result.astype(bf16),
            token_grad,
            modulator_grad,
            *attn_grads[:3],
            attn_grads[3].T,
            text_grads[:, :columns],
            text_grads[:, columns:],
            gate_grads,
            up_grads,
            down_grads.T,
            small[0],
            small[1],
            small[2],
            small[3],
            small[4],
            residual_rms,
        )

    return local


def solution(mesh):
    by_both = P(("fsdp", "seq"), None)
    return jax.shard_map(
        build(mesh.shape["fsdp"], mesh.shape["seq"]),
        mesh=mesh,
        in_specs=(
            by_both,
            by_both,
            P("fsdp", None),
            P("fsdp", None),
            P(None, "fsdp"),
            P("fsdp"),
            P("fsdp"),
            P("fsdp", "seq"),
            P("fsdp", "seq"),
            P("fsdp", "seq"),
            P("fsdp", "seq"),
            P("seq", "fsdp"),
            P("fsdp", "seq"),
            P("fsdp", "seq"),
            P("fsdp", "seq"),
            P("fsdp", "seq"),
            P("seq", "fsdp"),
            P(),
            P(),
            P(),
            P(),
            P(),
        ),
        out_specs=(
            by_both,
            by_both,
            P("fsdp", "seq"),
            P("fsdp", "seq"),
            P("fsdp", "seq"),
            P("fsdp", "seq"),
            P("seq", "fsdp"),
            P("fsdp", "seq"),
            P("fsdp", "seq"),
            P("fsdp", "seq"),
            P("fsdp", "seq"),
            P("seq", "fsdp"),
            P(),
            P(),
            P(),
            P(),
            P(),
            P(None, "fsdp"),
        ),
        check_vma=False,
    )
```

```python
import math

import jax
import jax.numpy as jnp
from jax import lax
from jax.experimental import pallas as pl
from jax.experimental.pallas import tpu as pltpu
from jax.sharding import PartitionSpec as P

epsilon = 1e-06
masked_score = -1e30
f32 = jnp.float32
bf16 = jnp.bfloat16


def rope_tables(positions, head_size):
    half = head_size // 2
    pair_index = jnp.arange(half)
    frequency = jnp.exp(pair_index.astype(f32) * (-2.0 * math.log(10000.0) / head_size))
    angle = jnp.zeros((positions.shape[1], half), f32)
    for axis_number in range(3):
        chosen = jnp.where(pair_index % 3 == axis_number, frequency, jnp.zeros_like(frequency))
        angle = angle + positions[axis_number].astype(f32)[:, None] * chosen[None, :]
    return (jnp.cos(angle), jnp.sin(angle))


def dot(left, right):
    return jnp.dot(left, right, preferred_element_type=f32)


def dot_nt(left, right):
    return lax.dot_general(left, right, (((1,), (1,)), ((), ())), preferred_element_type=f32)


def dot_tn(left, right):
    return lax.dot_general(left, right, (((0,), (0,)), ((), ())), preferred_element_type=f32)


def attention_forward(qkv, text, cosine, sine, gains, mask, text_mask, gate, heads, head):
    rows = qkv.shape[0]
    columns = heads * head
    block = min(rows, 256)

    def kernel(qkv_ref, text_ref, cos_ref, sin_ref, gain_ref, mask_ref, tmask_ref, gate_ref,
               q_ref, k_ref, v_ref, mixed_ref, cross_ref, lse_ref):
        cos = cos_ref[...]
        sin = sin_ref[...]
        lse_ref[...] = jnp.zeros_like(lse_ref)

        def turned(raw, gain):
            inverse = lax.rsqrt(jnp.mean(raw * raw, axis=-1, keepdims=True) + epsilon)
            value = raw * inverse * gain
            swapped = jnp.concatenate([value[:, head // 2 :], value[:, : head // 2]], axis=1)
            return (value * cos + swapped * sin).astype(bf16)

        for h in range(heads):
            at = slice(h * head, (h + 1) * head)
            q_ref[:, at] = turned(qkv_ref[:, at], gain_ref[0:1, :head])
            k_ref[:, at] = turned(
                qkv_ref[:, columns + h * head : columns + (h + 1) * head], gain_ref[1:2, :head]
            )
            v_ref[:, at] = qkv_ref[:, 2 * columns + h * head : 2 * columns + (h + 1) * head].astype(bf16)

        def attend(query, keys, values, masks):
            scores = dot_nt(query, keys) + masks
            peak = jnp.max(scores, axis=-1, keepdims=True)
            expo = jnp.exp(scores - peak)
            total = jnp.sum(expo, axis=-1, keepdims=True)
            return dot(expo.astype(bf16), values) / total, peak + jnp.log(total)

        for h in range(heads):
            at = slice(h * head, (h + 1) * head)
            keys = k_ref[:, at]
            values = v_ref[:, at]
            text_keys = text_ref[:, at]
            text_values = text_ref[:, columns + h * head : columns + (h + 1) * head]
            for b in range(rows // block):
                here = slice(b * block, (b + 1) * block)
                query = q_ref[here, at] * jnp.asarray(head**-0.5, bf16)
                own, own_lse = attend(query, keys, values, mask_ref[...])
                other, other_lse = attend(query, text_keys, text_values, tmask_ref[...])
                cross_ref[here, at] = other
                mixed_ref[here, at] = (own + gate_ref[:, at] * other).astype(bf16)
                lse_ref[here, h : h + 1] = own_lse
                lse_ref[here, heads + h : heads + h + 1] = other_lse

    wide = jax.ShapeDtypeStruct((rows, columns), bf16)
    return pl.pallas_call(
        kernel,
        out_shape=(wide, wide, wide, wide, jax.ShapeDtypeStruct((rows, columns), f32),
                   jax.ShapeDtypeStruct((rows, 128), f32)),
        in_specs=[pl.BlockSpec(memory_space=pltpu.VMEM)] * 8,
        out_specs=(pl.BlockSpec(memory_space=pltpu.VMEM),) * 6,
        compiler_params=pltpu.CompilerParams(vmem_limit_bytes=48 * 1024 * 1024),
        cost_estimate=pl.CostEstimate(
            flops=4 * rows * (rows + text.shape[0]) * columns,
            bytes_accessed=8 * rows * columns * 4,
            transcendentals=heads * rows * (rows + text.shape[0]),
        ),
        name="attention_forward",
    )(qkv, text, cosine, sine, gains, mask, text_mask, gate)


def soft_back(query, keys, values, masks, lse, back):
    probs = jnp.exp(dot_nt(query, keys) + masks - lse)
    grad_probs = dot_nt(back, values)
    delta = jnp.sum(probs * grad_probs, axis=-1, keepdims=True)
    return probs.astype(bf16), (probs * (grad_probs - delta)).astype(bf16)


def cross_backward(query, text, grad, lse, cross, text_mask, gate, heads, head):
    rows = query.shape[0]
    text_rows = text.shape[0]
    columns = heads * head
    block = min(rows, 256)
    scale = head**-0.5

    def kernel(q_ref, text_ref, grad_ref, lse_ref, cross_ref, tmask_ref, gate_ref,
               text_rows_ref, dq_ref, small_ref, dtk_ref, dtv_ref):
        small_ref[...] = jnp.zeros_like(small_ref)
        for h in range(heads):
            at = slice(h * head, (h + 1) * head)
            at_value = slice(columns + h * head, columns + (h + 1) * head)
            text_keys = text_ref[:, at]
            text_values = text_ref[:, at_value]
            for b in range(rows // block):
                here = slice(b * block, (b + 1) * block)
                query = q_ref[here, at] * jnp.asarray(scale, bf16)
                wide = grad_ref[here, at].astype(f32)
                cross_back = (wide * gate_ref[:, at]).astype(bf16)
                probs, grads = soft_back(
                    query, text_keys, text_values, tmask_ref[...],
                    lse_ref[here, heads + h : heads + h + 1], cross_back,
                )
                dq_ref[here, at] = dot(grads, text_keys)
                dtk = dot_tn(grads, query)
                dtv = dot_tn(probs, cross_back)
                small_ref[0:1, at] += jnp.sum(wide * cross_ref[here, at], axis=0, keepdims=True)
                if b == 0:
                    dtk_ref[...] = dtk
                    dtv_ref[...] = dtv
                else:
                    dtk_ref[...] += dtk
                    dtv_ref[...] += dtv
            text_rows_ref[:, at] = dtk_ref[...].astype(bf16)
            text_rows_ref[:, at_value] = dtv_ref[...].astype(bf16)

    return pl.pallas_call(
        kernel,
        out_shape=(
            jax.ShapeDtypeStruct((text_rows, 2 * columns), bf16),
            jax.ShapeDtypeStruct((rows, columns), f32),
            jax.ShapeDtypeStruct((8, columns), f32),
        ),
        in_specs=[pl.BlockSpec(memory_space=pltpu.VMEM)] * 7,
        out_specs=(pl.BlockSpec(memory_space=pltpu.VMEM),) * 3,
        scratch_shapes=[pltpu.VMEM((text_rows, head), f32)] * 2,
        compiler_params=pltpu.CompilerParams(vmem_limit_bytes=48 * 1024 * 1024),
        cost_estimate=pl.CostEstimate(
            flops=10 * rows * text_rows * columns,
            bytes_accessed=6 * rows * columns * 4,
            transcendentals=heads * rows * text_rows,
        ),
        name="cross_backward",
    )(query, text, grad, lse, cross, text_mask, gate)


def self_backward(qkv, query, key, value, grad, lse, cross_query, cosine, sine, gains, mask, heads, head):
    rows = qkv.shape[0]
    columns = heads * head
    block = min(rows, 256)
    scale = head**-0.5

    def kernel(qkv_ref, q_ref, k_ref, v_ref, grad_ref, lse_ref, cross_ref, cos_ref, sin_ref,
               gain_ref, mask_ref, rows_ref, small_ref, dq_ref, dk_ref, dv_ref):
        cos = cos_ref[...]
        sin = sin_ref[...]
        small_ref[...] = jnp.zeros_like(small_ref)

        def raw_back(grad, raw, gain, row):
            swapped = jnp.concatenate([grad[:, head // 2 :], grad[:, : head // 2]], axis=1)
            turned = grad * cos - swapped * sin
            inverse = lax.rsqrt(jnp.mean(raw * raw, axis=-1, keepdims=True) + epsilon)
            unit = raw * inverse
            small_ref[row : row + 1, :head] += jnp.sum(turned * unit, axis=0, keepdims=True)
            scaled = turned * gain
            return (
                inverse * (scaled - unit * jnp.mean(scaled * unit, axis=-1, keepdims=True))
            ).astype(bf16)

        for h in range(heads):
            at = slice(h * head, (h + 1) * head)
            at_key = slice(columns + h * head, columns + (h + 1) * head)
            at_value = slice(2 * columns + h * head, 2 * columns + (h + 1) * head)
            keys = k_ref[:, at]
            values = v_ref[:, at]
            for b in range(rows // block):
                here = slice(b * block, (b + 1) * block)
                query = q_ref[here, at] * jnp.asarray(scale, bf16)
                back = grad_ref[here, at]
                probs, grads = soft_back(
                    query, keys, values, mask_ref[...], lse_ref[here, h : h + 1], back
                )
                dq_ref[here, :] = (dot(grads, keys) + cross_ref[here, at]) * scale
                dk = dot_tn(grads, query)
                dv = dot_tn(probs, back)
                if b == 0:
                    dk_ref[...] = dk
                    dv_ref[...] = dv
                else:
                    dk_ref[...] += dk
                    dv_ref[...] += dv
            rows_ref[:, at] = raw_back(dq_ref[...], qkv_ref[:, at], gain_ref[0:1, :head], 0)
            rows_ref[:, at_key] = raw_back(dk_ref[...], qkv_ref[:, at_key], gain_ref[1:2, :head], 1)
            rows_ref[:, at_value] = dv_ref[...].astype(bf16)

    return pl.pallas_call(
        kernel,
        out_shape=(
            jax.ShapeDtypeStruct((rows, 3 * columns), bf16),
            jax.ShapeDtypeStruct((8, 128), f32),
        ),
        in_specs=[pl.BlockSpec(memory_space=pltpu.VMEM)] * 11,
        out_specs=(pl.BlockSpec(memory_space=pltpu.VMEM),) * 2,
        scratch_shapes=[pltpu.VMEM((rows, head), f32)] * 3,
        compiler_params=pltpu.CompilerParams(vmem_limit_bytes=48 * 1024 * 1024),
        cost_estimate=pl.CostEstimate(
            flops=10 * rows * rows * columns,
            bytes_accessed=10 * rows * columns * 4,
            transcendentals=heads * rows * rows,
        ),
        name="self_backward",
    )(qkv, query, key, value, grad, lse, cross_query, cosine, sine, gains, mask)


def ffn_forward(ffn_in, weights):
    rows, width = ffn_in.shape
    units = weights.shape[1] // 2
    tile = min(units, 256)
    tiles = units // tile

    def kernel(in_ref, gate_ref, up_ref, hidden_ref, by_gate_ref, by_up_ref):
        gate_act = dot(in_ref[...], gate_ref[...])
        up_act = dot(in_ref[...], up_ref[...])
        sigmoid = 1.0 / (1.0 + jnp.exp(-gate_act))
        silu = gate_act * sigmoid
        hidden_ref[...] = (silu * up_act).astype(bf16)
        by_gate_ref[...] = up_act * sigmoid * (1.0 + gate_act * (1.0 - sigmoid))
        by_up_ref[...] = silu

    part = pl.BlockSpec((rows, tile), lambda j: (0, j))
    wide = jax.ShapeDtypeStruct((rows, units), f32)
    return pl.pallas_call(
        kernel,
        grid=(tiles,),
        out_shape=(jax.ShapeDtypeStruct((rows, units), bf16), wide, wide),
        in_specs=[
            pl.BlockSpec((rows, width), lambda j: (0, 0)),
            pl.BlockSpec((width, tile), lambda j: (0, j)),
            pl.BlockSpec((width, tile), lambda j: (0, tiles + j)),
        ],
        out_specs=(part, part, part),
        compiler_params=pltpu.CompilerParams(vmem_limit_bytes=48 * 1024 * 1024),
        cost_estimate=pl.CostEstimate(
            flops=4 * rows * width * units,
            bytes_accessed=2 * rows * width + 4 * width * units + 10 * rows * units,
            transcendentals=rows * units,
        ),
        name="ffn_forward",
    )(ffn_in, weights, weights)


def ffn_backward(back, down, weights, by_gate, by_up):
    rows, width = back.shape
    units = down.shape[1]
    tile = min(units, 256)
    tiles = units // tile

    def kernel(back_ref, down_ref, gate_ref, up_ref, by_gate_ref, by_up_ref, act_ref, grad_ref, total):
        step = pl.program_id(0)

        @pl.when(step == 0)
        def _():
            total[...] = jnp.zeros_like(total)

        grad_hidden = dot(back_ref[...], down_ref[...])
        grad_gate = (grad_hidden * by_gate_ref[...]).astype(bf16)
        grad_up = (grad_hidden * by_up_ref[...]).astype(bf16)
        act_ref[:, pl.ds(pl.multiple_of(step * tile, tile), tile)] = grad_gate
        act_ref[:, pl.ds(pl.multiple_of(units + step * tile, tile), tile)] = grad_up
        total[...] += dot_nt(grad_gate, gate_ref[...]) + dot_nt(grad_up, up_ref[...])

        @pl.when(step == tiles - 1)
        def _():
            grad_ref[...] = total[...].astype(bf16)

    whole = pl.BlockSpec((rows, width), lambda j: (0, 0))
    part = pl.BlockSpec((rows, tile), lambda j: (0, j))
    return pl.pallas_call(
        kernel,
        grid=(tiles,),
        out_shape=(
            jax.ShapeDtypeStruct((rows, 2 * units), bf16),
            jax.ShapeDtypeStruct((rows, width), bf16),
        ),
        in_specs=[
            whole,
            pl.BlockSpec((width, tile), lambda j: (0, j)),
            pl.BlockSpec((width, tile), lambda j: (0, j)),
            pl.BlockSpec((width, tile), lambda j: (0, tiles + j)),
            part,
            part,
        ],
        out_specs=(pl.BlockSpec((rows, 2 * units), lambda j: (0, 0)), whole),
        scratch_shapes=[pltpu.VMEM((rows, width), f32)],
        compiler_params=pltpu.CompilerParams(vmem_limit_bytes=48 * 1024 * 1024),
        cost_estimate=pl.CostEstimate(
            flops=6 * rows * width * units,
            bytes_accessed=6 * rows * width + 6 * width * units + 12 * rows * units,
            transcendentals=0,
        ),
        name="ffn_backward",
    )(back, down, weights, weights, by_gate, by_up)


def widen(block, parts):
    rows = block.shape[0]
    columns = block.shape[1] // parts

    def kernel(block_ref, *part_refs):
        for i, part_ref in enumerate(part_refs):
            part_ref[...] = block_ref[:, i * columns : (i + 1) * columns].astype(f32)

    return pl.pallas_call(
        kernel,
        out_shape=[jax.ShapeDtypeStruct((rows, columns), f32)] * parts,
        in_specs=[pl.BlockSpec(memory_space=pltpu.VMEM)],
        out_specs=[pl.BlockSpec(memory_space=pltpu.VMEM)] * parts,
        name="widen",
    )(block)


def build(n_f, n_s):
    n_z = n_f // 2
    swaps = [[(i, i ^ k) for i in range(n_s)] for k in range(n_s)]

    def twin(block):
        return lax.ppermute(block, "fsdp", [(i, i ^ 1) for i in range(n_f)])

    def fsdp_xor(block, k):
        return lax.ppermute(block, "fsdp", [(i, i ^ k) for i in range(n_f)])

    def after(block, *earlier):
        return lax.optimization_barrier((block,) + earlier)[0]

    def stage(*values):
        return lax.optimization_barrier(values)

    def fsdp_scatter(total):
        return lax.psum_scatter(total, "fsdp", scatter_dimension=0, tiled=True)

    class Gather:
        def __init__(self, own, core):
            got = twin(own)
            first = core == 0
            pair = [jnp.where(first, own, got), jnp.where(first, got, own)]
            self.got = [jnp.concatenate(pair, axis=0)]
            self.twins = [None]

        def step(self, last=None):
            last = n_z - 1 if last is None else last
            while len(self.got) <= last:
                k = len(self.got)
                pairs = [(2 * z, 2 * z + 2) for z in range(k - 1, n_z - 1)]
                pairs += [(2 * z + 1, 2 * z - 1) for z in range(1, n_z - k + 1)]
                self.got.append(lax.ppermute(self.got[-1], "fsdp", pairs))

        def pass_on(self, last=None):
            last = n_z - 1 if last is None else last
            while len(self.twins) <= last:
                self.twins.append(twin(self.got[len(self.twins)]))

        def full(self, chip, core):
            rows, columns = self.got[0].shape
            whole = jnp.zeros((n_z, rows, columns), self.got[0].dtype)
            for k in range(n_z):
                block = self.got[0] if k == 0 else self.got[k] + self.twins[n_z - k]
                at = jnp.where(core == 0, lax.rem(chip + n_z - k, n_z), lax.rem(chip + k, n_z))
                whole = lax.dynamic_update_slice(whole, block[None], (at, 0, 0))
            return whole.reshape(n_z * rows, columns)

    def seq_near(block):
        return [lax.ppermute(block, "seq", swaps[k]) for k in (1, 2)]

    def seq_far(near, axis=0):
        half = near[0].shape[axis] // 2
        return [
            lax.ppermute(lax.slice_in_dim(near[0], 0, half, axis=axis), "seq", swaps[2]),
            lax.ppermute(lax.slice_in_dim(near[1], half, 2 * half, axis=axis), "seq", swaps[1]),
        ]

    def seq_gather(block, axis=0):
        if n_s != 4:
            parts = [block] + [lax.ppermute(block, "seq", swaps[k]) for k in range(1, n_s)]
        else:
            near = seq_near(block)
            far = jnp.concatenate(seq_far(near, axis + 1 if axis else 0), axis=axis + 1) if axis else None
            parts = [block] + near + ([far] if axis else seq_far(near))
        return jnp.concatenate(parts, axis=axis)

    def seq_send(total, rows):
        return [
            lax.ppermute(total[k * rows : (k + 1) * rows].astype(bf16), "seq", swaps[k])
            for k in range(1, n_s)
        ]

    def seq_sum(total, parts, rows):
        result = total[:rows].astype(f32)
        for part in parts:
            result = result + part.astype(f32)
        return result

    def by_seq(stacked, index):
        bit = 1
        while bit < n_s:
            split = stacked.reshape((n_s // (2 * bit), 2, bit) + stacked.shape[1:])
            turn = (index & bit) != 0
            first = jnp.where(turn, split[:, 1], split[:, 0])
            second = jnp.where(turn, split[:, 0], split[:, 1])
            stacked = jnp.stack([first, second], axis=1).reshape(stacked.shape)
            bit *= 2
        return stacked

    def all_sum(block, axis, size):
        bit = 1
        while bit < size:
            block = block + lax.ppermute(block, axis, [(i, i ^ bit) for i in range(size)])
            bit *= 2
        return block

    def local(
        tokens,
        cotangent,
        condition,
        caption,
        positions,
        clip_lengths,
        caption_lengths,
        modulator,
        query_weight,
        key_weight,
        value_weight,
        output_weight,
        textkey_weight,
        textvalue_weight,
        gate_weight,
        up_weight,
        down_weight,
        attn_gain,
        ffn_gain,
        query_gain,
        key_gain,
        cross_gate,
    ):
        rows = tokens.shape[0]
        width = tokens.shape[1]
        head_size = query_gain.shape[0]
        columns = query_weight.shape[1]
        heads = columns // head_size
        units = gate_weight.shape[1]
        clip_rows = positions.shape[1]
        text_rows = caption.shape[0]
        seq_index = lax.axis_index("seq")
        fsdp_index = lax.axis_index("fsdp")
        length = clip_lengths[0]
        text_length = caption_lengths[0]
        scale = head_size ** (-0.5)

        chip = fsdp_index // 2
        core = fsdp_index % 2

        def fsdp_gather(*parts):
            return lax.all_gather(jnp.concatenate(parts, axis=1), "fsdp", axis=0, tiled=True)

        attn_full = fsdp_gather(query_weight, key_weight, value_weight, output_weight.T)
        qkv_full = attn_full[:, : 3 * columns]
        output_t = attn_full[:, 3 * columns :]
        cap_rows = text_rows // n_s
        cap_columns = textkey_weight.shape[0]
        cap_piece = lax.dynamic_slice_in_dim(caption, seq_index * cap_rows, cap_rows, 0)
        cap_mine = cap_piece.reshape(cap_rows, n_f, cap_columns).transpose(1, 0, 2)
        cap_mine = lax.all_to_all(cap_mine, "fsdp", 0, 0)
        cond_low = jax.nn.silu(after(condition, cap_mine).astype(f32)).astype(bf16)
        cond_all = cond_low
        bit = 1
        while bit < n_f:
            cond_all = jnp.concatenate([cond_all, fsdp_xor(cond_all, bit)], axis=0)
            bit *= 2
        tokens_all = seq_gather(tokens)
        mod_rows = modulator.shape[0]
        cond_mine = lax.dynamic_slice_in_dim(cond_all, fsdp_index * mod_rows, mod_rows, 1)
        mod_part = dot(cond_mine, modulator)
        half = n_f // 2
        while half:
            mod_part = mod_part[:half] + fsdp_xor(mod_part[half:], half)
            half //= 2
        cap_all = seq_gather(cap_mine[:, None], 1)
        modulation = mod_part
        bit = 1
        while bit < n_s:
            modulation = jnp.concatenate(
                [modulation, lax.ppermute(modulation, "seq", swaps[bit])], axis=0
            )
            bit *= 2
        modulation = by_seq(modulation, seq_index).reshape(-1)
        cap_all = cap_all.reshape(n_f * text_rows, cap_columns)
        text_own = jnp.concatenate([textkey_weight, textvalue_weight], axis=1)
        text_part = dot(cap_all, text_own).astype(bf16)
        text_both = fsdp_scatter(text_part)
        ffn_full = fsdp_gather(after(gate_weight, text_part), up_weight)
        down_t = lax.all_gather(down_weight.T, "fsdp", axis=0, tiled=True)
        tokens_all = tokens_all.astype(f32)
        cotangent_all = seq_gather(after(cotangent, cap_all)).astype(f32)

        scale_attn = modulation[:width]
        gate_attn = modulation[width : 2 * width]
        scale_ffn = modulation[2 * width : 3 * width]
        gate_ffn = modulation[3 * width :]
        tanh_attn = jnp.tanh(gate_attn)
        tanh_ffn = jnp.tanh(gate_ffn)

        order = [seq_index ^ k for k in range(n_s)]
        row_index = jnp.concatenate([order[k] * rows + jnp.arange(rows) for k in range(n_s)])
        text_index = jnp.concatenate(
            [order[k] * cap_rows + jnp.arange(cap_rows) for k in range(n_s)]
        )
        places = jnp.concatenate(
            [lax.dynamic_slice_in_dim(positions, order[k] * rows, rows, 1) for k in range(n_s)],
            axis=1,
        )

        inv_attn_all = lax.rsqrt(jnp.mean(tokens_all * tokens_all, axis=-1, keepdims=True) + epsilon)
        normed_all = (tokens_all * inv_attn_all * attn_gain * (1.0 + scale_attn)).astype(bf16)
        inputs = tokens.astype(f32)
        inv_attn = inv_attn_all[:rows]
        unit_attn = inputs * inv_attn
        qkv = dot(normed_all, qkv_full)
        cosine, sine = rope_tables(places, head_size)
        cosine = jnp.concatenate([cosine, cosine], axis=1)
        sine = jnp.concatenate([-sine, sine], axis=1)
        gains = jnp.zeros((8, head_size), f32).at[0].set(query_gain).at[1].set(key_gain)
        mask = jnp.where(row_index < length, 0.0, masked_score).astype(f32)[None, :]
        text_mask = jnp.where(text_index < text_length, 0.0, masked_score).astype(f32)[None, :]
        gate_heads = jnp.tanh(lax.dynamic_slice_in_dim(cross_gate, seq_index * heads, heads))
        gate_row = jnp.repeat(gate_heads, head_size)[None, :]
        query_rot, key_rot, value_low, mixed_rows, cross_out, lse = attention_forward(
            qkv, text_both, cosine, sine, gains, mask, text_mask, gate_row, heads, head_size
        )
        attn_sent = dot_nt(mixed_rows, output_t)
        attn_out = seq_sum(attn_sent, seq_send(attn_sent, rows), rows)
        branch_attn = tanh_attn * attn_out
        hidden_in = inputs + branch_attn
        inv_ffn = lax.rsqrt(jnp.mean(hidden_in * hidden_in, axis=-1, keepdims=True) + epsilon)
        unit_ffn = hidden_in * inv_ffn
        ffn_in = (unit_ffn * ffn_gain * (1.0 + scale_ffn)).astype(bf16)
        ffn_all = seq_gather(ffn_in)
        ffn_back_all = (tanh_ffn * cotangent_all).astype(bf16)
        hidden, by_gate, by_up = ffn_forward(ffn_all, ffn_full)
        down_part = dot_tn(ffn_back_all, hidden).astype(bf16)
        down_grads = fsdp_scatter(down_part)
        grad_act, grad_sent = ffn_backward(
            ffn_back_all, after(down_t, down_part), ffn_full, by_gate, by_up
        )
        parts = seq_send(grad_sent, rows)
        act_part = dot_tn(ffn_all, grad_act).astype(bf16)
        *parts, act_part = stage(*parts, act_part)
        grad_ffn_in = seq_sum(grad_sent, parts, rows)
        grad_out = cotangent.astype(f32)
        grad_ffn_gain = jnp.sum(grad_ffn_in * unit_ffn * (1.0 + scale_ffn), axis=0)
        grad_scale_ffn = jnp.sum(grad_ffn_in * unit_ffn * ffn_gain, axis=0)
        scaled_ffn = grad_ffn_in * ffn_gain * (1.0 + scale_ffn)
        grad_hidden_in = grad_out + inv_ffn * (
            scaled_ffn - unit_ffn * jnp.mean(scaled_ffn * unit_ffn, axis=-1, keepdims=True)
        )
        attn_back = (tanh_attn * grad_hidden_in).astype(bf16)
        grad_gate_attn = jnp.sum(grad_hidden_in * attn_out, axis=0) * (1.0 - tanh_attn * tanh_attn)
        attn_back, act_part = stage(attn_back, act_part)
        act_grads = fsdp_scatter(after(act_part, down_grads))
        attn_back_all = seq_gather(attn_back)
        grad_mixed = dot(attn_back_all, output_t).astype(bf16)
        output_part = dot_tn(attn_back_all, mixed_rows).astype(bf16)
        ffn_sent = dot_nt(after(hidden, attn_back_all), down_t)
        ffn_parts = seq_send(ffn_sent, rows)
        text_grads_rows, cross_query, gate_sums = cross_backward(
            query_rot, text_both, grad_mixed, lse, cross_out, text_mask, gate_row, heads, head_size
        )
        text_back = Gather(text_grads_rows, core)
        cross_query, text_back.got[0] = stage(cross_query, text_back.got[0])
        text_back.step(1)
        qkv_rows, head_sums = self_backward(
            qkv, query_rot, key_rot, value_low, grad_mixed, lse, cross_query,
            cosine, sine, gains, mask, heads, head_size,
        )
        qkv_rows, text_back.got[1], *ffn_parts = stage(qkv_rows, text_back.got[1], *ffn_parts)
        text_back.step(2)
        text_back.pass_on(1)
        normed_sent = dot_nt(qkv_rows, qkv_full)
        parts = seq_send(normed_sent, rows)
        qkv_part = dot_tn(normed_all, after(qkv_rows, normed_sent)).astype(bf16)
        qkv_part, text_back.got[2], text_back.twins[1] = stage(
            qkv_part, text_back.got[2], text_back.twins[1]
        )
        text_back.step()
        text_back.pass_on(2)
        attn_part = jnp.concatenate([qkv_part, output_part], axis=1)
        ffn_out = seq_sum(ffn_sent, ffn_parts, rows)
        branch_ffn = tanh_ffn * ffn_out
        result = hidden_in + branch_ffn
        row_valid = (seq_index * rows + jnp.arange(rows) < length)[:, None]
        sums = jnp.stack(
            [
                jnp.sum(jnp.where(row_valid, result * result, 0.0)),
                jnp.sum(jnp.where(row_valid, branch_attn * branch_attn, 0.0)),
                jnp.sum(jnp.where(row_valid, branch_ffn * branch_ffn, 0.0)),
            ]
        )
        grad_gate_ffn = jnp.sum(grad_out * ffn_out, axis=0) * (1.0 - tanh_ffn * tanh_ffn)

        grad_query_gain = head_sums[0, :head_size]
        grad_key_gain = head_sums[1, :head_size]
        grad_gate_heads = jnp.sum(
            gate_sums[0].reshape(heads, head_size), axis=1
        ) * (1.0 - gate_heads * gate_heads)
        attn_part, act_grads, parts[0] = stage(attn_part, act_grads, parts[0])
        attn_grads = fsdp_scatter(attn_part)
        act_grads = widen(act_grads, 2)
        down_grads = widen(down_grads, 1)[0]
        *parts, down_grads, gate_grads, up_grads, text_back.got[-1] = stage(
            *parts, down_grads, *act_grads, text_back.got[-1]
        )
        text_back.pass_on()
        grad_normed = seq_sum(normed_sent, parts, rows)
        grad_attn_gain = jnp.sum(grad_normed * unit_attn * (1.0 + scale_attn), axis=0)
        grad_scale_attn = jnp.sum(grad_normed * unit_attn * attn_gain, axis=0)
        scaled_attn = grad_normed * attn_gain * (1.0 + scale_attn)
        token_grad = grad_hidden_in + inv_attn * (
            scaled_attn - unit_attn * jnp.mean(scaled_attn * unit_attn, axis=-1, keepdims=True)
        )

        gate_heads_full = lax.dynamic_update_slice_in_dim(
            jnp.zeros_like(cross_gate), grad_gate_heads, seq_index * heads, 0
        )
        sizes = jnp.concatenate(
            [grad_attn_gain, grad_ffn_gain, gate_heads_full, grad_query_gain, grad_key_gain, sums]
        )
        sizes = all_sum(sizes, "seq", n_s)
        mod_grad = jnp.concatenate([grad_scale_attn, grad_gate_attn, grad_scale_ffn, grad_gate_ffn])
        mod_mine = by_seq(mod_grad.reshape(n_s, -1), seq_index)
        half = n_s // 2
        while half:
            mod_mine = mod_mine[:half] + lax.ppermute(mod_mine[half:], "seq", swaps[half])
            half //= 2
        text_grads = dot_tn(cap_all, text_back.full(chip, core))
        mod_mine = mod_mine.astype(bf16)
        bit = 1
        while bit < n_f:
            mod_mine = jnp.concatenate([mod_mine, fsdp_xor(mod_mine, bit)], axis=0)
            bit *= 2
        modulator_grad = dot_tn(cond_mine, mod_mine)
        totals = sizes[-3:]
        residual_rms = jnp.sqrt(totals / (length.astype(f32) * width))[:, None]
        small = all_sum(sizes[:-3], "fsdp", n_f)
        attn_grads = widen(attn_grads, 4)
        n_heads = cross_gate.shape[0]
        ends = [width, width, n_heads, head_size, head_size]
        ends = [sum(ends[:i]) for i in range(6)]
        small = [small[ends[i] : ends[i + 1]] for i in range(5)]
        small = (small[0], small[1], small[3], small[4], small[2])
        return (
            result.astype(bf16),
            token_grad,
            modulator_grad,
            *attn_grads[:3],
            attn_grads[3].T,
            text_grads[:, :columns],
            text_grads[:, columns:],
            gate_grads,
            up_grads,
            down_grads.T,
            small[0],
            small[1],
            small[2],
            small[3],
            small[4],
            residual_rms,
        )

    return local


def solution(mesh):
    by_both = P(("fsdp", "seq"), None)
    return jax.shard_map(
        build(mesh.shape["fsdp"], mesh.shape["seq"]),
        mesh=mesh,
        in_specs=(
            by_both,
            by_both,
            P("fsdp", None),
            P("fsdp", None),
            P(None, "fsdp"),
            P("fsdp"),
            P("fsdp"),
            P("fsdp", "seq"),
            P("fsdp", "seq"),
            P("fsdp", "seq"),
            P("fsdp", "seq"),
            P("seq", "fsdp"),
            P("fsdp", "seq"),
            P("fsdp", "seq"),
            P("fsdp", "seq"),
            P("fsdp", "seq"),
            P("seq", "fsdp"),
            P(),
            P(),
            P(),
            P(),
            P(),
        ),
        out_specs=(
            by_both,
            by_both,
            P("fsdp", "seq"),
            P("fsdp", "seq"),
            P("fsdp", "seq"),
            P("fsdp", "seq"),
            P("seq", "fsdp"),
            P("fsdp", "seq"),
            P("fsdp", "seq"),
            P("fsdp", "seq"),
            P("fsdp", "seq"),
            P("seq", "fsdp"),
            P(),
            P(),
            P(),
            P(),
            P(),
            P(None, "fsdp"),
        ),
        check_vma=False,
    )
```

```python
import math

import jax
import jax.numpy as jnp
from jax import lax
from jax.experimental import pallas as pl
from jax.experimental.pallas import tpu as pltpu
from jax.sharding import PartitionSpec as P

epsilon = 1e-06
masked_score = -1e30
f32 = jnp.float32
bf16 = jnp.bfloat16


def rope_tables(positions, head_size):
    half = head_size // 2
    pair_index = jnp.arange(half)
    frequency = jnp.exp(pair_index.astype(f32) * (-2.0 * math.log(10000.0) / head_size))
    angle = jnp.zeros((positions.shape[1], half), f32)
    for axis_number in range(3):
        chosen = jnp.where(pair_index % 3 == axis_number, frequency, jnp.zeros_like(frequency))
        angle = angle + positions[axis_number].astype(f32)[:, None] * chosen[None, :]
    return (jnp.cos(angle), jnp.sin(angle))


def dot(left, right):
    return jnp.dot(left, right, preferred_element_type=f32)


def dot_nt(left, right):
    return lax.dot_general(left, right, (((1,), (1,)), ((), ())), preferred_element_type=f32)


def dot_tn(left, right):
    return lax.dot_general(left, right, (((0,), (0,)), ((), ())), preferred_element_type=f32)


def attention_forward(qkv, text, cosine, sine, gains, mask, text_mask, gate, heads, head):
    rows = qkv.shape[0]
    columns = heads * head
    block = min(rows, 256)

    def kernel(qkv_ref, text_ref, cos_ref, sin_ref, gain_ref, mask_ref, tmask_ref, gate_ref,
               q_ref, k_ref, v_ref, mixed_ref, cross_ref, lse_ref):
        cos = cos_ref[...]
        sin = sin_ref[...]
        lse_ref[...] = jnp.zeros_like(lse_ref)

        def turned(raw, gain):
            inverse = lax.rsqrt(jnp.mean(raw * raw, axis=-1, keepdims=True) + epsilon)
            value = raw * inverse * gain
            swapped = jnp.concatenate([value[:, head // 2 :], value[:, : head // 2]], axis=1)
            return (value * cos + swapped * sin).astype(bf16)

        for h in range(heads):
            at = slice(h * head, (h + 1) * head)
            q_ref[:, at] = turned(qkv_ref[:, at], gain_ref[0:1, :head])
            k_ref[:, at] = turned(
                qkv_ref[:, columns + h * head : columns + (h + 1) * head], gain_ref[1:2, :head]
            )
            v_ref[:, at] = qkv_ref[:, 2 * columns + h * head : 2 * columns + (h + 1) * head].astype(bf16)

        def attend(query, keys, values, masks):
            scores = dot_nt(query, keys) + masks
            peak = jnp.max(scores, axis=-1, keepdims=True)
            expo = jnp.exp(scores - peak)
            total = jnp.sum(expo, axis=-1, keepdims=True)
            return dot(expo.astype(bf16), values) / total, peak + jnp.log(total)

        for h in range(heads):
            at = slice(h * head, (h + 1) * head)
            keys = k_ref[:, at]
            values = v_ref[:, at]
            text_keys = text_ref[:, at]
            text_values = text_ref[:, columns + h * head : columns + (h + 1) * head]
            for b in range(rows // block):
                here = slice(b * block, (b + 1) * block)
                query = q_ref[here, at] * jnp.asarray(head**-0.5, bf16)
                own, own_lse = attend(query, keys, values, mask_ref[...])
                other, other_lse = attend(query, text_keys, text_values, tmask_ref[...])
                cross_ref[here, at] = other
                mixed_ref[here, at] = (own + gate_ref[:, at] * other).astype(bf16)
                lse_ref[here, h : h + 1] = own_lse
                lse_ref[here, heads + h : heads + h + 1] = other_lse

    wide = jax.ShapeDtypeStruct((rows, columns), bf16)
    return pl.pallas_call(
        kernel,
        out_shape=(wide, wide, wide, wide, jax.ShapeDtypeStruct((rows, columns), f32),
                   jax.ShapeDtypeStruct((rows, 128), f32)),
        in_specs=[pl.BlockSpec(memory_space=pltpu.VMEM)] * 8,
        out_specs=(pl.BlockSpec(memory_space=pltpu.VMEM),) * 6,
        compiler_params=pltpu.CompilerParams(vmem_limit_bytes=48 * 1024 * 1024),
        cost_estimate=pl.CostEstimate(
            flops=4 * rows * (rows + text.shape[0]) * columns,
            bytes_accessed=8 * rows * columns * 4,
            transcendentals=heads * rows * (rows + text.shape[0]),
        ),
        name="attention_forward",
    )(qkv, text, cosine, sine, gains, mask, text_mask, gate)


def soft_back(query, keys, values, masks, lse, back):
    probs = jnp.exp(dot_nt(query, keys) + masks - lse)
    grad_probs = dot_nt(back, values)
    delta = jnp.sum(probs * grad_probs, axis=-1, keepdims=True)
    return probs.astype(bf16), (probs * (grad_probs - delta)).astype(bf16)


def cross_backward(query, text, grad, lse, cross, text_mask, gate, heads, head):
    rows = query.shape[0]
    text_rows = text.shape[0]
    columns = heads * head
    block = min(rows, 256)
    scale = head**-0.5

    def kernel(q_ref, text_ref, grad_ref, lse_ref, cross_ref, tmask_ref, gate_ref,
               text_rows_ref, dq_ref, small_ref, dtk_ref, dtv_ref):
        small_ref[...] = jnp.zeros_like(small_ref)
        for h in range(heads):
            at = slice(h * head, (h + 1) * head)
            at_value = slice(columns + h * head, columns + (h + 1) * head)
            text_keys = text_ref[:, at]
            text_values = text_ref[:, at_value]
            for b in range(rows // block):
                here = slice(b * block, (b + 1) * block)
                query = q_ref[here, at] * jnp.asarray(scale, bf16)
                wide = grad_ref[here, at].astype(f32)
                cross_back = (wide * gate_ref[:, at]).astype(bf16)
                probs, grads = soft_back(
                    query, text_keys, text_values, tmask_ref[...],
                    lse_ref[here, heads + h : heads + h + 1], cross_back,
                )
                dq_ref[here, at] = dot(grads, text_keys)
                dtk = dot_tn(grads, query)
                dtv = dot_tn(probs, cross_back)
                small_ref[0:1, at] += jnp.sum(wide * cross_ref[here, at], axis=0, keepdims=True)
                if b == 0:
                    dtk_ref[...] = dtk
                    dtv_ref[...] = dtv
                else:
                    dtk_ref[...] += dtk
                    dtv_ref[...] += dtv
            text_rows_ref[:, at] = dtk_ref[...].astype(bf16)
            text_rows_ref[:, at_value] = dtv_ref[...].astype(bf16)

    return pl.pallas_call(
        kernel,
        out_shape=(
            jax.ShapeDtypeStruct((text_rows, 2 * columns), bf16),
            jax.ShapeDtypeStruct((rows, columns), f32),
            jax.ShapeDtypeStruct((8, columns), f32),
        ),
        in_specs=[pl.BlockSpec(memory_space=pltpu.VMEM)] * 7,
        out_specs=(pl.BlockSpec(memory_space=pltpu.VMEM),) * 3,
        scratch_shapes=[pltpu.VMEM((text_rows, head), f32)] * 2,
        compiler_params=pltpu.CompilerParams(vmem_limit_bytes=48 * 1024 * 1024),
        cost_estimate=pl.CostEstimate(
            flops=10 * rows * text_rows * columns,
            bytes_accessed=6 * rows * columns * 4,
            transcendentals=heads * rows * text_rows,
        ),
        name="cross_backward",
    )(query, text, grad, lse, cross, text_mask, gate)


def self_backward(qkv, query, key, value, grad, lse, cross_query, cosine, sine, gains, mask, heads, head):
    rows = qkv.shape[0]
    columns = heads * head
    block = min(rows, 256)
    scale = head**-0.5

    def kernel(qkv_ref, q_ref, k_ref, v_ref, grad_ref, lse_ref, cross_ref, cos_ref, sin_ref,
               gain_ref, mask_ref, rows_ref, small_ref, dq_ref, dk_ref, dv_ref):
        cos = cos_ref[...]
        sin = sin_ref[...]
        small_ref[...] = jnp.zeros_like(small_ref)

        def raw_back(grad, raw, gain, row):
            swapped = jnp.concatenate([grad[:, head // 2 :], grad[:, : head // 2]], axis=1)
            turned = grad * cos - swapped * sin
            inverse = lax.rsqrt(jnp.mean(raw * raw, axis=-1, keepdims=True) + epsilon)
            unit = raw * inverse
            small_ref[row : row + 1, :head] += jnp.sum(turned * unit, axis=0, keepdims=True)
            scaled = turned * gain
            return (
                inverse * (scaled - unit * jnp.mean(scaled * unit, axis=-1, keepdims=True))
            ).astype(bf16)

        for h in range(heads):
            at = slice(h * head, (h + 1) * head)
            at_key = slice(columns + h * head, columns + (h + 1) * head)
            at_value = slice(2 * columns + h * head, 2 * columns + (h + 1) * head)
            keys = k_ref[:, at]
            values = v_ref[:, at]
            for b in range(rows // block):
                here = slice(b * block, (b + 1) * block)
                query = q_ref[here, at] * jnp.asarray(scale, bf16)
                back = grad_ref[here, at]
                probs, grads = soft_back(
                    query, keys, values, mask_ref[...], lse_ref[here, h : h + 1], back
                )
                dq_ref[here, :] = (dot(grads, keys) + cross_ref[here, at]) * scale
                dk = dot_tn(grads, query)
                dv = dot_tn(probs, back)
                if b == 0:
                    dk_ref[...] = dk
                    dv_ref[...] = dv
                else:
                    dk_ref[...] += dk
                    dv_ref[...] += dv
            rows_ref[:, at] = raw_back(dq_ref[...], qkv_ref[:, at], gain_ref[0:1, :head], 0)
            rows_ref[:, at_key] = raw_back(dk_ref[...], qkv_ref[:, at_key], gain_ref[1:2, :head], 1)
            rows_ref[:, at_value] = dv_ref[...].astype(bf16)

    return pl.pallas_call(
        kernel,
        out_shape=(
            jax.ShapeDtypeStruct((rows, 3 * columns), bf16),
            jax.ShapeDtypeStruct((8, 128), f32),
        ),
        in_specs=[pl.BlockSpec(memory_space=pltpu.VMEM)] * 11,
        out_specs=(pl.BlockSpec(memory_space=pltpu.VMEM),) * 2,
        scratch_shapes=[pltpu.VMEM((rows, head), f32)] * 3,
        compiler_params=pltpu.CompilerParams(vmem_limit_bytes=48 * 1024 * 1024),
        cost_estimate=pl.CostEstimate(
            flops=10 * rows * rows * columns,
            bytes_accessed=10 * rows * columns * 4,
            transcendentals=heads * rows * rows,
        ),
        name="self_backward",
    )(qkv, query, key, value, grad, lse, cross_query, cosine, sine, gains, mask)


def ffn_forward(ffn_in, weights, units):
    rows, width = ffn_in.shape
    tile = min(units, 256)
    tiles = units // tile

    def kernel(in_ref, gate_ref, up_ref, hidden_ref, by_gate_ref, by_up_ref):
        gate_act = dot(in_ref[...], gate_ref[...])
        up_act = dot(in_ref[...], up_ref[...])
        sigmoid = 1.0 / (1.0 + jnp.exp(-gate_act))
        silu = gate_act * sigmoid
        hidden_ref[...] = (silu * up_act).astype(bf16)
        by_gate_ref[...] = up_act * sigmoid * (1.0 + gate_act * (1.0 - sigmoid))
        by_up_ref[...] = silu

    part = pl.BlockSpec((rows, tile), lambda j: (0, j))
    wide = jax.ShapeDtypeStruct((rows, units), f32)
    return pl.pallas_call(
        kernel,
        grid=(tiles,),
        out_shape=(jax.ShapeDtypeStruct((rows, units), bf16), wide, wide),
        in_specs=[
            pl.BlockSpec((rows, width), lambda j: (0, 0)),
            pl.BlockSpec((width, tile), lambda j: (0, j)),
            pl.BlockSpec((width, tile), lambda j: (0, tiles + j)),
        ],
        out_specs=(part, part, part),
        compiler_params=pltpu.CompilerParams(vmem_limit_bytes=48 * 1024 * 1024),
        cost_estimate=pl.CostEstimate(
            flops=4 * rows * width * units,
            bytes_accessed=2 * rows * width + 4 * width * units + 10 * rows * units,
            transcendentals=rows * units,
        ),
        name="ffn_forward",
    )(ffn_in, weights, weights)


def ffn_backward(back, weights, by_gate, by_up):
    rows, width = back.shape
    units = by_up.shape[1]
    tile = min(units, 256)
    tiles = units // tile

    def kernel(back_ref, down_ref, gate_ref, up_ref, by_gate_ref, by_up_ref, act_ref, grad_ref, total):
        step = pl.program_id(0)

        @pl.when(step == 0)
        def _():
            total[...] = jnp.zeros_like(total)

        grad_hidden = dot(back_ref[...], down_ref[...])
        grad_gate = (grad_hidden * by_gate_ref[...]).astype(bf16)
        grad_up = (grad_hidden * by_up_ref[...]).astype(bf16)
        act_ref[:, pl.ds(pl.multiple_of(step * tile, tile), tile)] = grad_gate
        act_ref[:, pl.ds(pl.multiple_of(units + step * tile, tile), tile)] = grad_up
        total[...] += dot_nt(grad_gate, gate_ref[...]) + dot_nt(grad_up, up_ref[...])

        @pl.when(step == tiles - 1)
        def _():
            grad_ref[...] = total[...].astype(bf16)

    whole = pl.BlockSpec((rows, width), lambda j: (0, 0))
    part = pl.BlockSpec((rows, tile), lambda j: (0, j))
    return pl.pallas_call(
        kernel,
        grid=(tiles,),
        out_shape=(
            jax.ShapeDtypeStruct((rows, 2 * units), bf16),
            jax.ShapeDtypeStruct((rows, width), bf16),
        ),
        in_specs=[
            whole,
            pl.BlockSpec((width, tile), lambda j: (0, 2 * tiles + j)),
            pl.BlockSpec((width, tile), lambda j: (0, j)),
            pl.BlockSpec((width, tile), lambda j: (0, tiles + j)),
            part,
            part,
        ],
        out_specs=(pl.BlockSpec((rows, 2 * units), lambda j: (0, 0)), whole),
        scratch_shapes=[pltpu.VMEM((rows, width), f32)],
        compiler_params=pltpu.CompilerParams(vmem_limit_bytes=48 * 1024 * 1024),
        cost_estimate=pl.CostEstimate(
            flops=6 * rows * width * units,
            bytes_accessed=6 * rows * width + 6 * width * units + 12 * rows * units,
            transcendentals=0,
        ),
        name="ffn_backward",
    )(back, weights, weights, weights, by_gate, by_up)


def widen(block, parts):
    rows = block.shape[0]
    columns = block.shape[1] // parts

    def kernel(block_ref, *part_refs):
        for i, part_ref in enumerate(part_refs):
            part_ref[...] = block_ref[:, i * columns : (i + 1) * columns].astype(f32)

    return pl.pallas_call(
        kernel,
        out_shape=[jax.ShapeDtypeStruct((rows, columns), f32)] * parts,
        in_specs=[pl.BlockSpec(memory_space=pltpu.VMEM)],
        out_specs=[pl.BlockSpec(memory_space=pltpu.VMEM)] * parts,
        name="widen",
    )(block)


def build(n_f, n_s):
    n_z = n_f // 2
    swaps = [[(i, i ^ k) for i in range(n_s)] for k in range(n_s)]

    def twin(block):
        return lax.ppermute(block, "fsdp", [(i, i ^ 1) for i in range(n_f)])

    def fsdp_xor(block, k):
        return lax.ppermute(block, "fsdp", [(i, i ^ k) for i in range(n_f)])

    def after(block, *earlier):
        return lax.optimization_barrier((block,) + earlier)[0]

    def stage(*values):
        return lax.optimization_barrier(values)

    def fsdp_scatter(total):
        return lax.psum_scatter(total, "fsdp", scatter_dimension=0, tiled=True)

    class Gather:
        def __init__(self, own, core):
            got = twin(own)
            first = core == 0
            pair = [jnp.where(first, own, got), jnp.where(first, got, own)]
            self.got = [jnp.concatenate(pair, axis=0)]
            self.twins = [None]

        def step(self, last=None):
            last = n_z - 1 if last is None else last
            while len(self.got) <= last:
                k = len(self.got)
                pairs = [(2 * z, 2 * z + 2) for z in range(k - 1, n_z - 1)]
                pairs += [(2 * z + 1, 2 * z - 1) for z in range(1, n_z - k + 1)]
                self.got.append(lax.ppermute(self.got[-1], "fsdp", pairs))

        def pass_on(self, last=None):
            last = n_z - 1 if last is None else last
            while len(self.twins) <= last:
                self.twins.append(twin(self.got[len(self.twins)]))

        def full(self, chip, core):
            rows, columns = self.got[0].shape
            whole = jnp.zeros((n_z, rows, columns), self.got[0].dtype)
            for k in range(n_z):
                block = self.got[0] if k == 0 else self.got[k] + self.twins[n_z - k]
                at = jnp.where(core == 0, lax.rem(chip + n_z - k, n_z), lax.rem(chip + k, n_z))
                whole = lax.dynamic_update_slice(whole, block[None], (at, 0, 0))
            return whole.reshape(n_z * rows, columns)

    def seq_near(block):
        return [lax.ppermute(block, "seq", swaps[k]) for k in (1, 2)]

    def seq_far(near, axis=0):
        half = near[0].shape[axis] // 2
        return [
            lax.ppermute(lax.slice_in_dim(near[0], 0, half, axis=axis), "seq", swaps[2]),
            lax.ppermute(lax.slice_in_dim(near[1], half, 2 * half, axis=axis), "seq", swaps[1]),
        ]

    def seq_gather(block, axis=0):
        if n_s != 4:
            parts = [block] + [lax.ppermute(block, "seq", swaps[k]) for k in range(1, n_s)]
        else:
            near = seq_near(block)
            far = jnp.concatenate(seq_far(near, axis + 1 if axis else 0), axis=axis + 1) if axis else None
            parts = [block] + near + ([far] if axis else seq_far(near))
        return jnp.concatenate(parts, axis=axis)

    def seq_send(total, rows):
        return [
            lax.ppermute(total[k * rows : (k + 1) * rows].astype(bf16), "seq", swaps[k])
            for k in range(1, n_s)
        ]

    def seq_sum(total, parts, rows):
        result = total[:rows].astype(f32)
        for part in parts:
            result = result + part.astype(f32)
        return result

    def by_seq(stacked, index):
        bit = 1
        while bit < n_s:
            split = stacked.reshape((n_s // (2 * bit), 2, bit) + stacked.shape[1:])
            turn = (index & bit) != 0
            first = jnp.where(turn, split[:, 1], split[:, 0])
            second = jnp.where(turn, split[:, 0], split[:, 1])
            stacked = jnp.stack([first, second], axis=1).reshape(stacked.shape)
            bit *= 2
        return stacked

    def all_sum(block, axis, size):
        bit = 1
        while bit < size:
            block = block + lax.ppermute(block, axis, [(i, i ^ bit) for i in range(size)])
            bit *= 2
        return block

    def local(
        tokens,
        cotangent,
        condition,
        caption,
        positions,
        clip_lengths,
        caption_lengths,
        modulator,
        query_weight,
        key_weight,
        value_weight,
        output_weight,
        textkey_weight,
        textvalue_weight,
        gate_weight,
        up_weight,
        down_weight,
        attn_gain,
        ffn_gain,
        query_gain,
        key_gain,
        cross_gate,
    ):
        rows = tokens.shape[0]
        width = tokens.shape[1]
        head_size = query_gain.shape[0]
        columns = query_weight.shape[1]
        heads = columns // head_size
        units = gate_weight.shape[1]
        clip_rows = positions.shape[1]
        text_rows = caption.shape[0]
        seq_index = lax.axis_index("seq")
        fsdp_index = lax.axis_index("fsdp")
        length = clip_lengths[0]
        text_length = caption_lengths[0]
        scale = head_size ** (-0.5)

        chip = fsdp_index // 2
        core = fsdp_index % 2

        def fsdp_gather(*parts):
            return lax.all_gather(jnp.concatenate(parts, axis=1), "fsdp", axis=0, tiled=True)

        attn_full = fsdp_gather(query_weight, key_weight, value_weight, output_weight.T)
        qkv_full = attn_full[:, : 3 * columns]
        output_t = attn_full[:, 3 * columns :]
        cap_rows = text_rows // n_s
        cap_columns = textkey_weight.shape[0]
        cap_piece = lax.dynamic_slice_in_dim(caption, seq_index * cap_rows, cap_rows, 0)
        cap_mine = cap_piece.reshape(cap_rows, n_f, cap_columns).transpose(1, 0, 2)
        cap_mine = lax.all_to_all(cap_mine, "fsdp", 0, 0)
        cond_low = jax.nn.silu(after(condition, cap_mine).astype(f32)).astype(bf16)
        cond_all = cond_low
        bit = 1
        while bit < n_f:
            cond_all = jnp.concatenate([cond_all, fsdp_xor(cond_all, bit)], axis=0)
            bit *= 2
        tokens_all = seq_gather(tokens)
        mod_rows = modulator.shape[0]
        cond_mine = lax.dynamic_slice_in_dim(cond_all, fsdp_index * mod_rows, mod_rows, 1)
        mod_part = dot(cond_mine, modulator)
        half = n_f // 2
        while half:
            mod_part = mod_part[:half] + fsdp_xor(mod_part[half:], half)
            half //= 2
        cap_all = seq_gather(cap_mine[:, None], 1)
        modulation = mod_part
        bit = 1
        while bit < n_s:
            modulation = jnp.concatenate(
                [modulation, lax.ppermute(modulation, "seq", swaps[bit])], axis=0
            )
            bit *= 2
        modulation = by_seq(modulation, seq_index).reshape(-1)
        cap_all = cap_all.reshape(n_f * text_rows, cap_columns)
        text_own = jnp.concatenate([textkey_weight, textvalue_weight], axis=1)
        text_part = dot(cap_all, text_own).astype(bf16)
        text_both = fsdp_scatter(text_part)
        ffn_full = fsdp_gather(after(gate_weight, text_part), up_weight, down_weight.T)
        down_t = ffn_full[:, 2 * units :]
        tokens_all = tokens_all.astype(f32)
        cotangent_all = seq_gather(after(cotangent, cap_all)).astype(f32)

        scale_attn = modulation[:width]
        gate_attn = modulation[width : 2 * width]
        scale_ffn = modulation[2 * width : 3 * width]
        gate_ffn = modulation[3 * width :]
        tanh_attn = jnp.tanh(gate_attn)
        tanh_ffn = jnp.tanh(gate_ffn)

        order = [seq_index ^ k for k in range(n_s)]
        row_index = jnp.concatenate([order[k] * rows + jnp.arange(rows) for k in range(n_s)])
        text_index = jnp.concatenate(
            [order[k] * cap_rows + jnp.arange(cap_rows) for k in range(n_s)]
        )
        places = jnp.concatenate(
            [lax.dynamic_slice_in_dim(positions, order[k] * rows, rows, 1) for k in range(n_s)],
            axis=1,
        )

        inv_attn_all = lax.rsqrt(jnp.mean(tokens_all * tokens_all, axis=-1, keepdims=True) + epsilon)
        normed_all = (tokens_all * inv_attn_all * attn_gain * (1.0 + scale_attn)).astype(bf16)
        inputs = tokens.astype(f32)
        inv_attn = inv_attn_all[:rows]
        unit_attn = inputs * inv_attn
        qkv = dot(normed_all, qkv_full)
        cosine, sine = rope_tables(places, head_size)
        cosine = jnp.concatenate([cosine, cosine], axis=1)
        sine = jnp.concatenate([-sine, sine], axis=1)
        gains = jnp.zeros((8, head_size), f32).at[0].set(query_gain).at[1].set(key_gain)
        mask = jnp.where(row_index < length, 0.0, masked_score).astype(f32)[None, :]
        text_mask = jnp.where(text_index < text_length, 0.0, masked_score).astype(f32)[None, :]
        gate_heads = jnp.tanh(lax.dynamic_slice_in_dim(cross_gate, seq_index * heads, heads))
        gate_row = jnp.repeat(gate_heads, head_size)[None, :]
        query_rot, key_rot, value_low, mixed_rows, cross_out, lse = attention_forward(
            qkv, text_both, cosine, sine, gains, mask, text_mask, gate_row, heads, head_size
        )
        attn_sent = dot_nt(mixed_rows, output_t)
        attn_out = seq_sum(attn_sent, seq_send(attn_sent, rows), rows)
        branch_attn = tanh_attn * attn_out
        hidden_in = inputs + branch_attn
        inv_ffn = lax.rsqrt(jnp.mean(hidden_in * hidden_in, axis=-1, keepdims=True) + epsilon)
        unit_ffn = hidden_in * inv_ffn
        ffn_in = (unit_ffn * ffn_gain * (1.0 + scale_ffn)).astype(bf16)
        ffn_all = seq_gather(ffn_in)
        ffn_back_all = (tanh_ffn * cotangent_all).astype(bf16)
        hidden, by_gate, by_up = ffn_forward(ffn_all, ffn_full, units)
        down_part = dot_tn(ffn_back_all, hidden).astype(bf16)
        down_grads = fsdp_scatter(down_part)
        grad_act, grad_sent = ffn_backward(
            after(ffn_back_all, down_part), ffn_full, by_gate, by_up
        )
        parts = seq_send(grad_sent, rows)
        act_part = dot_tn(ffn_all, grad_act).astype(bf16)
        *parts, act_part = stage(*parts, act_part)
        grad_ffn_in = seq_sum(grad_sent, parts, rows)
        grad_out = cotangent.astype(f32)
        grad_ffn_gain = jnp.sum(grad_ffn_in * unit_ffn * (1.0 + scale_ffn), axis=0)
        grad_scale_ffn = jnp.sum(grad_ffn_in * unit_ffn * ffn_gain, axis=0)
        scaled_ffn = grad_ffn_in * ffn_gain * (1.0 + scale_ffn)
        grad_hidden_in = grad_out + inv_ffn * (
            scaled_ffn - unit_ffn * jnp.mean(scaled_ffn * unit_ffn, axis=-1, keepdims=True)
        )
        attn_back = (tanh_attn * grad_hidden_in).astype(bf16)
        grad_gate_attn = jnp.sum(grad_hidden_in * attn_out, axis=0) * (1.0 - tanh_attn * tanh_attn)
        attn_back, act_part = stage(attn_back, act_part)
        act_grads = fsdp_scatter(after(act_part, down_grads))
        attn_back_all = seq_gather(attn_back)
        grad_mixed = dot(attn_back_all, output_t).astype(bf16)
        output_part = dot_tn(attn_back_all, mixed_rows).astype(bf16)
        ffn_sent = dot_nt(after(hidden, attn_back_all), down_t)
        ffn_parts = seq_send(ffn_sent, rows)
        text_grads_rows, cross_query, gate_sums = cross_backward(
            query_rot, text_both, grad_mixed, lse, cross_out, text_mask, gate_row, heads, head_size
        )
        text_back = Gather(text_grads_rows, core)
        cross_query, text_back.got[0] = stage(cross_query, text_back.got[0])
        text_back.step(1)
        qkv_rows, head_sums = self_backward(
            qkv, query_rot, key_rot, value_low, grad_mixed, lse, cross_query,
            cosine, sine, gains, mask, heads, head_size,
        )
        qkv_rows, text_back.got[1], *ffn_parts = stage(qkv_rows, text_back.got[1], *ffn_parts)
        text_back.step(2)
        text_back.pass_on(1)
        normed_sent = dot_nt(qkv_rows, qkv_full)
        parts = seq_send(normed_sent, rows)
        qkv_part = dot_tn(normed_all, after(qkv_rows, normed_sent)).astype(bf16)
        qkv_part, text_back.got[2], text_back.twins[1] = stage(
            qkv_part, text_back.got[2], text_back.twins[1]
        )
        text_back.step()
        text_back.pass_on(2)
        attn_part = jnp.concatenate([qkv_part, output_part], axis=1)
        ffn_out = seq_sum(ffn_sent, ffn_parts, rows)
        branch_ffn = tanh_ffn * ffn_out
        result = hidden_in + branch_ffn
        row_valid = (seq_index * rows + jnp.arange(rows) < length)[:, None]
        sums = jnp.stack(
            [
                jnp.sum(jnp.where(row_valid, result * result, 0.0)),
                jnp.sum(jnp.where(row_valid, branch_attn * branch_attn, 0.0)),
                jnp.sum(jnp.where(row_valid, branch_ffn * branch_ffn, 0.0)),
            ]
        )
        grad_gate_ffn = jnp.sum(grad_out * ffn_out, axis=0) * (1.0 - tanh_ffn * tanh_ffn)

        grad_query_gain = head_sums[0, :head_size]
        grad_key_gain = head_sums[1, :head_size]
        grad_gate_heads = jnp.sum(
            gate_sums[0].reshape(heads, head_size), axis=1
        ) * (1.0 - gate_heads * gate_heads)
        attn_part, act_grads, text_back.got[-1], parts[0] = stage(
            attn_part, act_grads, text_back.got[-1], parts[0]
        )
        text_back.pass_on()
        text_grads = dot_tn(cap_all, text_back.full(chip, core))
        attn_grads = fsdp_scatter(attn_part)
        act_grads = widen(act_grads, 2)
        down_grads = widen(down_grads, 1)[0]
        *parts, text_grads, down_grads, gate_grads, up_grads = stage(
            *parts, text_grads, down_grads, *act_grads
        )
        grad_normed = seq_sum(normed_sent, parts, rows)
        grad_attn_gain = jnp.sum(grad_normed * unit_attn * (1.0 + scale_attn), axis=0)
        grad_scale_attn = jnp.sum(grad_normed * unit_attn * attn_gain, axis=0)
        scaled_attn = grad_normed * attn_gain * (1.0 + scale_attn)
        token_grad = grad_hidden_in + inv_attn * (
            scaled_attn - unit_attn * jnp.mean(scaled_attn * unit_attn, axis=-1, keepdims=True)
        )

        gate_heads_full = lax.dynamic_update_slice_in_dim(
            jnp.zeros_like(cross_gate), grad_gate_heads, seq_index * heads, 0
        )
        sizes = jnp.concatenate(
            [grad_attn_gain, grad_ffn_gain, gate_heads_full, grad_query_gain, grad_key_gain, sums]
        )
        sizes = all_sum(sizes, "seq", n_s)
        mod_grad = jnp.concatenate([grad_scale_attn, grad_gate_attn, grad_scale_ffn, grad_gate_ffn])
        mod_mine = by_seq(mod_grad.reshape(n_s, -1), seq_index)
        half = n_s // 2
        while half:
            mod_mine = mod_mine[:half] + lax.ppermute(mod_mine[half:], "seq", swaps[half])
            half //= 2
        mod_mine = mod_mine.astype(bf16)
        bit = 1
        while bit < n_f:
            mod_mine = jnp.concatenate([mod_mine, fsdp_xor(mod_mine, bit)], axis=0)
            bit *= 2
        modulator_grad = dot_tn(cond_mine, mod_mine)
        totals = sizes[-3:]
        residual_rms = jnp.sqrt(totals / (length.astype(f32) * width))[:, None]
        small = all_sum(sizes[:-3], "fsdp", n_f)
        attn_grads = widen(attn_grads, 4)
        n_heads = cross_gate.shape[0]
        ends = [width, width, n_heads, head_size, head_size]
        ends = [sum(ends[:i]) for i in range(6)]
        small = [small[ends[i] : ends[i + 1]] for i in range(5)]
        small = (small[0], small[1], small[3], small[4], small[2])
        return (
            result.astype(bf16),
            token_grad,
            modulator_grad,
            *attn_grads[:3],
            attn_grads[3].T,
            text_grads[:, :columns],
            text_grads[:, columns:],
            gate_grads,
            up_grads,
            down_grads.T,
            small[0],
            small[1],
            small[2],
            small[3],
            small[4],
            residual_rms,
        )

    return local


def solution(mesh):
    by_both = P(("fsdp", "seq"), None)
    return jax.shard_map(
        build(mesh.shape["fsdp"], mesh.shape["seq"]),
        mesh=mesh,
        in_specs=(
            by_both,
            by_both,
            P("fsdp", None),
            P("fsdp", None),
            P(None, "fsdp"),
            P("fsdp"),
            P("fsdp"),
            P("fsdp", "seq"),
            P("fsdp", "seq"),
            P("fsdp", "seq"),
            P("fsdp", "seq"),
            P("seq", "fsdp"),
            P("fsdp", "seq"),
            P("fsdp", "seq"),
            P("fsdp", "seq"),
            P("fsdp", "seq"),
            P("seq", "fsdp"),
            P(),
            P(),
            P(),
            P(),
            P(),
        ),
        out_specs=(
            by_both,
            by_both,
            P("fsdp", "seq"),
            P("fsdp", "seq"),
            P("fsdp", "seq"),
            P("fsdp", "seq"),
            P("seq", "fsdp"),
            P("fsdp", "seq"),
            P("fsdp", "seq"),
            P("fsdp", "seq"),
            P("fsdp", "seq"),
            P("seq", "fsdp"),
            P(),
            P(),
            P(),
            P(),
            P(),
            P(None, "fsdp"),
        ),
        check_vma=False,
    )
```
